32 devices in a mesh: group: 2 (over x), scan: 16 (over z, y, core).
Axes of the slice: x: 2, y: 2, z: 4, core: 2. Of those that a mesh axis runs over, the one named last changes fastest.
Arguments:
- object_blocks: float32 [1024, 8, 1024], P(('group', 'scan')), parts along dimension 0, may hold values from -2 to 2
- probe: float32 [4, 256, 256], P('group'), parts along dimension 0, may hold values from -6 to 6
- positions: int32 [64, 2], P(('group', 'scan')), parts along dimension 0, may hold values from 0 to 256
- anchors: int32 [32, 2], P(('group', 'scan')), parts along dimension 0, may hold values from 0 to 16, as said below
- amplitudes: float32 [64, 256, 256], P(('group', 'scan')), parts along dimension 0, may hold values from 0.1 to 3
Outputs:
- object_gradient: float32 [1024, 8, 1024], P(('group', 'scan')), parts along dimension 0
- probe_gradient: float32 [4, 256, 256], P('group'), parts along dimension 0
The draws below stay inside these ranges and needn't reach their ends.
There are 2 independent parts, one for each index of `group`. The reference program is written for one: setup_inputs(seed, part) draws one part's arguments, and reference() takes and returns one part's arrays. A program takes and returns all parts, laid end to end along the dimension named above; each array names one. Nothing has to cross between parts.
Inputs may be any that keep to these rules, and one draw needn't show every extreme that they name: `anchors`: each device's footprint of 16 x 16 blocks lies inside the region: block rows up to 0, block columns up to 16. `positions`: rows p * 2 to p * 2 + 1 belong to device p, and give offsets from that device's anchors times 32.
All inputs are finite; a program needn't handle non-finite values.
Results may differ from the reference program's by a relative error of at most 0.017.
Values may be sent and summed in bfloat16 or wider, within the bound.
No kernel may reach another device: no remote copies, remote signals or barrier semaphores. Data moves between devices by JAX's collectives and lax.ppermute only.
A program may use at most 192 MiB of HBM per device.

```python
import math
import jax
import jax.numpy as jnp
from jax import lax

PATCH = 256
SLICES = 4
BSIDE = 32
FOOT = 16
OWN_COLS = 16
COL_BANDS = 2
P_DEV = 2
OWN_ROWS = 1
BLK_DEV = 32
BLOCKS = 512
BLOCK_ROWS = 16
BLOCK_COLS = 32
POSITIONS = 32
BB = 1024
N_SCAN = 16


def draw_anchors(key, part):
    key = jax.random.fold_in(key, 3)
    row_key, col_key = jax.random.split(key)
    row_top = jax.random.randint(row_key, (N_SCAN,), 0, BLOCK_ROWS - FOOT + 1)
    col_top = jax.random.randint(col_key, (N_SCAN,), 0, BLOCK_COLS - FOOT + 1)
    row_top = row_top.at[0].set(BLOCK_ROWS - FOOT).at[1].set(0)
    col_top = col_top.at[0].set(BLOCK_COLS - FOOT).at[1].set(0)
    return jnp.stack([row_top, col_top], axis=1).astype(jnp.int32)


def with_ends(result, key, smallest, high):
    spot = [jax.random.randint(jax.random.fold_in(key, axis), (), 0, length) for axis, length in enumerate(result.shape)]
    main_axis = result.shape.index(max(result.shape))
    neighbour = spot[:main_axis] + [(spot[main_axis] + 1) % result.shape[main_axis]] + spot[main_axis + 1:]
    return result.at[tuple(spot)].set(smallest).at[tuple(neighbour)].set(high)


def block_scale(stream_key, extent, cuts, least, largest):
    level, own = 1.0, jax.random.fold_in(stream_key, 6)
    for dim, parts in cuts:
        draws = jnp.exp(jax.random.uniform(jax.random.fold_in(own, dim), (parts,), jnp.float32, least / len(cuts), largest / len(cuts)))
        level = level * jnp.repeat(draws, extent[dim] // parts).reshape([-1 if axis == dim else 1 for axis in range(len(extent))])
    return level


def scatter_about(rng, extent, scale, bound, cuts=(), kind=jnp.bfloat16):
    loudness = block_scale(rng, extent, cuts, -0.22, 0.18) if cuts else 1.0
    values = jax.random.normal(rng, extent, jnp.float32) * scale * loudness
    return jnp.minimum(jnp.maximum(values, -bound), bound).astype(kind)


def setup_inputs(seed: int = 0, part: int = 0) -> dict:
    seeds = jax.random.split(jax.random.key(seed), 6)
    part_keys = jax.random.split(jax.random.fold_in(seeds[5], part), 6)
    return {
        "object_blocks": scatter_about(part_keys[0], (BLOCKS, 2 * SLICES, BB), 0.3, 2.0, ((0, 16),), jnp.float32),
        "probe": scatter_about(part_keys[1], (2, PATCH, PATCH), 1.0, 6.0, (), jnp.float32),
        "positions": with_ends(jax.random.randint(part_keys[2], (POSITIONS, 2), 0, FOOT * BSIDE - PATCH + 1), jax.random.fold_in(part_keys[2], 1), 0, FOOT * BSIDE - PATCH).astype(jnp.int32),
        "anchors": draw_anchors(jax.random.fold_in(jax.random.fold_in(seeds[5], part), 71), part),
        "amplitudes": jnp.clip(jnp.exp(math.log(3.0) - 3.4011974 * jax.random.uniform(part_keys[4], (POSITIONS, PATCH, PATCH), jnp.float32) ** block_scale(part_keys[4], (POSITIONS, PATCH, PATCH), ((0, 16),), -0.2, 0.2)), 0.1, 3.0),
    }


FLOOR = 0.25

def matmul_f32(left_op, right_op):
    return jnp.dot(left_op, right_op, preferred_element_type=jnp.float32)

def dft_table():
    counter = jnp.arange(PATCH, dtype=jnp.int32)
    turns = counter[:, None] * counter[None, :] % PATCH
    angles = turns.astype(jnp.float32) * (2.0 * math.pi / PATCH)
    scaled = 1.0 / math.sqrt(PATCH)
    return ((jnp.cos(angles) * scaled).astype(jnp.bfloat16), (-jnp.sin(angles) * scaled).astype(jnp.bfloat16))

def circulant(kernel):
    tiled = jnp.tile(kernel, PATCH + 1)[:PATCH * (PATCH + 1)]
    summed_index = tiled.reshape(PATCH, PATCH + 1)[:, :PATCH]
    return jnp.roll(summed_index[:, ::-1], 1, axis=1)

def fresnel_table():
    counter = jnp.arange(PATCH, dtype=jnp.int32)
    centred = (counter + PATCH // 2) % PATCH - PATCH // 2
    turns = (4 * counter[:, None] * counter[None, :] - centred[None, :] * centred[None, :]) % (4 * PATCH)
    angles = turns.astype(jnp.float32) * (2.0 * math.pi / (4 * PATCH))
    kernel_real = (lax.optimization_barrier(jnp.sum(jnp.cos(angles), axis=1)) / PATCH).astype(jnp.bfloat16)
    kernel_imag = (lax.optimization_barrier(jnp.sum(jnp.sin(angles), axis=1)) / PATCH).astype(jnp.bfloat16)
    return (circulant(kernel_real), circulant(kernel_imag))

def conjugate(table):
    return (table[0], -table[1])

def to_bf16(pair):
    return (pair[0].astype(jnp.bfloat16), pair[1].astype(jnp.bfloat16))

def product_left(table, wavefield):
    real_part = matmul_f32(table[0], wavefield[0]) - matmul_f32(table[1], wavefield[1])
    imag_part = matmul_f32(table[0], wavefield[1]) + matmul_f32(table[1], wavefield[0])
    return (real_part, imag_part)

def product_right(wavefield, table):
    real_part = matmul_f32(wavefield[0], table[0]) - matmul_f32(wavefield[1], table[1])
    imag_part = matmul_f32(wavefield[0], table[1]) + matmul_f32(wavefield[1], table[0])
    return (real_part, imag_part)

def sandwich(table_left, wavefield, table_right):
    half_way = to_bf16(product_left(table_left, wavefield))
    return product_right(half_way, table_right)

def one_position(patch, probe, measured, dft, fresnel):
    trans_real = 1.0 + patch[0::2].astype(jnp.float32)
    trans_imag = patch[1::2].astype(jnp.float32)
    probe_real = probe[0]
    probe_imag = probe[1]
    wavefield = to_bf16((probe_real * trans_real[0] - probe_imag * trans_imag[0], probe_real * trans_imag[0] + probe_imag * trans_real[0]))
    carried = []
    for layer in range(1, SLICES):
        spread = to_bf16(sandwich(fresnel, wavefield, fresnel))
        carried.append(spread)
        spread_real = spread[0].astype(jnp.float32)
        spread_imag = spread[1].astype(jnp.float32)
        wavefield = to_bf16((trans_real[layer] * spread_real - trans_imag[layer] * spread_imag, trans_real[layer] * spread_imag + trans_imag[layer] * spread_real))
    far_real, far_imag = sandwich(dft, wavefield, dft)
    modulus = jnp.sqrt(far_real * far_real + far_imag * far_imag)
    keeping = 1.0 - measured / jnp.maximum(modulus, FLOOR)
    misfit = to_bf16((far_real * keeping, far_imag * keeping))
    back_dft = conjugate(dft)
    back_fresnel = conjugate(fresnel)
    adjoint = to_bf16(sandwich(back_dft, misfit, back_dft))
    slice_grads = [None] * SLICES
    for layer in range(SLICES - 1, 0, -1):
        spread_real = carried[layer - 1][0].astype(jnp.float32)
        spread_imag = carried[layer - 1][1].astype(jnp.float32)
        adj_real = adjoint[0].astype(jnp.float32)
        adj_imag = adjoint[1].astype(jnp.float32)
        slice_grads[layer] = (adj_real * spread_real + adj_imag * spread_imag, adj_imag * spread_real - adj_real * spread_imag)
        before = to_bf16((trans_real[layer] * adj_real + trans_imag[layer] * adj_imag, trans_real[layer] * adj_imag - trans_imag[layer] * adj_real))
        adjoint = to_bf16(sandwich(back_fresnel, before, back_fresnel))
    adj_real = adjoint[0].astype(jnp.float32)
    adj_imag = adjoint[1].astype(jnp.float32)
    slice_grads[0] = (adj_real * probe_real + adj_imag * probe_imag, adj_imag * probe_real - adj_real * probe_imag)
    probe_grad = jnp.stack([adj_real * trans_real[0] + adj_imag * trans_imag[0], adj_imag * trans_real[0] - adj_real * trans_imag[0]])
    stacked = jnp.stack([member for pair in slice_grads for member in pair])
    return (stacked, probe_grad)

def block_grid():
    row_block = jnp.arange(BLOCK_ROWS, dtype=jnp.int32)[:, None]
    col_block = jnp.arange(BLOCK_COLS, dtype=jnp.int32)[None, :]
    holder = row_block % OWN_ROWS * OWN_COLS + col_block % OWN_COLS
    local = row_block // OWN_ROWS * COL_BANDS + col_block // OWN_COLS
    return (holder * BLK_DEV + local).reshape(-1)

def block_places():
    numbers = jnp.arange(BLOCKS, dtype=jnp.int32)
    holder = numbers // BLK_DEV
    local = numbers % BLK_DEV
    row_block = local // COL_BANDS * OWN_ROWS + holder // OWN_COLS
    col_block = local % COL_BANDS * OWN_COLS + holder % OWN_COLS
    return row_block * BLOCK_COLS + col_block

def reference(object_blocks, probe, positions, anchors, amplitudes):
    channels = 2 * SLICES
    stored = object_blocks.astype(jnp.bfloat16)
    gridded = jnp.take(stored, block_grid(), axis=0).reshape(BLOCK_ROWS, BLOCK_COLS, channels, BSIDE, BSIDE)
    image = gridded.transpose(2, 0, 3, 1, 4).reshape(channels, BLOCK_ROWS * BSIDE, BLOCK_COLS * BSIDE)
    dft = dft_table()
    fresnel = fresnel_table()
    device_of = jnp.arange(POSITIONS, dtype=jnp.int32) // P_DEV
    corners = (positions + jnp.take(anchors, device_of, axis=0) * BSIDE).astype(jnp.int32)
    root = jnp.zeros((), jnp.int32)

    def visit(carry, item):
        grad_image, probe_total = carry
        corner, measured = item
        starts = (root, corner[0], corner[1])
        patch = lax.dynamic_slice(image, starts, (channels, PATCH, PATCH))
        slice_grads, probe_grad = one_position(patch, probe, measured, dft, fresnel)
        window = lax.dynamic_slice(grad_image, starts, (channels, PATCH, PATCH))
        grad_image = lax.dynamic_update_slice(grad_image, window + slice_grads, starts)
        return ((grad_image, probe_total + probe_grad), None)
    begin = (jnp.zeros((channels, BLOCK_ROWS * BSIDE, BLOCK_COLS * BSIDE), jnp.float32), jnp.zeros((2, PATCH, PATCH), jnp.float32))
    (grad_image, probe_total), unused = lax.scan(visit, begin, (corners, amplitudes))
    blocked = grad_image.reshape(channels, BLOCK_ROWS, BSIDE, BLOCK_COLS, BSIDE).transpose(1, 3, 0, 2, 4)
    blocked = blocked.reshape(BLOCK_ROWS * BLOCK_COLS, channels, BSIDE * BSIDE)
    object_gradient = jnp.take(blocked, block_places(), axis=0)
    probe_gradient = probe_total / math.sqrt(POSITIONS)
    return (object_gradient, probe_gradient)
```

```python
import math

import jax
import jax.numpy as jnp
import numpy as np
from jax import lax
from jax.experimental import pallas as pl
from jax.experimental.pallas import tpu as pltpu
from jax.sharding import PartitionSpec as P

PATCH = 256
SLICES = 4
BSIDE = 32
FOOT = 16
OWN_COLS = 16
COL_BANDS = 2
FLOOR = 0.25
WIN = 9
TALL = FOOT * BSIDE
VMEM_BYTES = 48 * 1024 * 1024
F32 = jnp.float32
BF16 = jnp.bfloat16


def lane_rows():
    lane = np.arange(PATCH)
    return lane % 8 * BSIDE + lane // 8


def stacked_right(table):
    real, imag = table
    return np.block([[real, imag], [-imag, real]])


def stacked_left(table):
    real, imag = table
    return np.block([[real, -imag], [imag, real]])


def tables():
    counter = np.arange(PATCH)
    turns = counter[:, None] * counter[None, :] % PATCH
    angles = turns.astype(np.float64) * (2.0 * math.pi / PATCH)
    scaled = 1.0 / math.sqrt(PATCH)
    dft = (np.cos(angles) * scaled, -np.sin(angles) * scaled)
    centred = (counter + PATCH // 2) % PATCH - PATCH // 2
    turns = (4 * counter[:, None] * counter[None, :] - centred[None, :] ** 2) % (4 * PATCH)
    angles = turns.astype(np.float64) * (2.0 * math.pi / (4 * PATCH))
    gap = (counter[:, None] - counter[None, :]) % PATCH
    fresnel = ((np.cos(angles).sum(1) / PATCH)[gap], (np.sin(angles).sum(1) / PATCH)[gap])
    order = lane_rows()
    across = tuple(part.T[np.ix_(order, order)] for part in fresnel)
    down = tuple(part.T for part in fresnel)
    wanted = (
        stacked_right(across),
        stacked_left(down),
        stacked_left(dft),
        stacked_right(dft),
    )
    return tuple(jnp.asarray(t.astype(np.float32)).astype(BF16) for t in wanted)


def dot(left, right):
    return jnp.dot(left, right, preferred_element_type=F32)


def dot_nt(left, right):
    return lax.dot_general(left, right, (((1,), (1,)), ((), ())), preferred_element_type=F32)


def row_of_lane(shape):
    lane = lax.broadcasted_iota(jnp.int32, shape, 1)
    return (lane & 7) * BSIDE + (lane >> 3)


def shifts(meta, p, dtype=BF16):
    top, left = meta[p, 0], meta[p, 1]
    shape = (PATCH, PATCH)
    i = lax.broadcasted_iota(jnp.int32, shape, 0)
    j = lax.broadcasted_iota(jnp.int32, shape, 1)
    my = jnp.where(row_of_lane(shape) == ((i + top) & (PATCH - 1)), 1.0, 0.0).astype(dtype)
    mx = jnp.where(i == ((j + left) & (PATCH - 1)), 1.0, 0.0).astype(dtype)
    return my, mx


def cols(c):
    return pl.ds(c * PATCH, PATCH)


def fetch(meta, sources, window, sems, patches):
    per = sources[0].shape[0]

    def copy(source, place, p, k):
        return pltpu.make_async_copy(source.at[place], window.at[p, k], sems.at[p, k])

    for p in range(patches):
        for k in range(WIN):
            place = meta[p, 2 + k]
            for n, source in enumerate(sources):

                @pl.when(place // per == n)
                def _(source=source, place=place, n=n, p=p, k=k):
                    copy(source, place - n * per, p, k).start()

    for p in range(patches):
        for k in range(WIN):
            copy(sources[0], 0, p, k).wait()


def patch_rows(meta, window, p, k):
    top, left = meta[p, 0], meta[p, 1]
    low = row_of_lane((BSIDE, PATCH)) < top
    out = []
    for c in range(2):

        def pick(slot):
            strip = window[p, slot, c].astype(F32)
            return jnp.where(low, strip[:, PATCH:], strip[:, :PATCH])

        value = pick(k)
        if k == 0:
            b = lax.broadcasted_iota(jnp.int32, (BSIDE, PATCH), 0)
            value = jnp.where(b < left, pick(WIN - 1), value)
        out.append(value)
    return out


def propagate(field, half, right, left, patches, put):
    for p in range(patches):
        y = dot(field[cols(p), :], right[...])
        for c in range(2):
            half[cols(c), cols(p)] = y[:, c * PATCH : (c + 1) * PATCH].astype(BF16)
    for c in range(2):
        put(c, dot(left[cols(c), :], half[...]))


def add_gradient(meta, grid, p, k, pair):
    top, left = meta[p, 0], meta[p, 1]
    low = row_of_lane((BSIDE, PATCH)) < top
    b = lax.broadcasted_iota(jnp.int32, (BSIDE, PATCH), 0)

    def put(slot, c, value):
        place = meta[p, 2 + WIN + slot]
        for half in range(2):
            piece = jnp.where(low if half else jnp.logical_not(low), value, 0.0)
            spot = (place, c, slice(None), slice(half * PATCH, (half + 1) * PATCH))
            if p > 0 or slot == WIN - 1:
                piece = piece + grid[spot].astype(F32)
            grid[spot] = piece.astype(BF16)

    if k > 0:
        for c in range(2):
            put(k, c, pair[c])
        return
    for c in range(2):
        put(0, c, jnp.where(b < left, 0.0, pair[c]))

    @pl.when(left > 0)
    def _():
        for c in range(2):
            put(WIN - 1, c, jnp.where(b < left, pair[c], 0.0))


def send_out(grid, outs, sems):
    start = 0
    copies = []
    for n, out in enumerate(outs):
        size = out.shape[0]
        copies.append(pltpu.make_async_copy(grid.at[pl.ds(start, size)], out, sems.at[n]))
        start += size
    for copy in copies:
        copy.start()
    return copies


def rows(k):
    return pl.ds(k * BSIDE, BSIDE)


def at_rows(c, k):
    return pl.ds(c * PATCH + k * BSIDE, BSIDE)


def any_spec():
    return pl.BlockSpec(memory_space=pl.ANY)


def vmem_spec():
    return pl.BlockSpec(memory_space=pltpu.VMEM)


def smem_spec():
    return pl.BlockSpec(memory_space=pltpu.SMEM)


def params():
    return pltpu.CompilerParams(vmem_limit_bytes=VMEM_BYTES)


def cost(products, bytes_accessed):
    return pl.CostEstimate(
        flops=products * 8 * PATCH**3, bytes_accessed=bytes_accessed, transcendentals=0
    )


def wrap_probe(meta, probe, patches):
    def kernel(meta, probe, out):
        for p in range(patches):
            my, mx = shifts(meta, p, F32)
            for c in range(2):
                half = lax.dot_general(
                    mx,
                    probe[c],
                    (((1,), (1,)), ((), ())),
                    precision=lax.Precision.HIGHEST,
                    preferred_element_type=F32,
                )
                out[p, c] = jnp.dot(
                    half, my, precision=lax.Precision.HIGHEST, preferred_element_type=F32
                )

    return pl.pallas_call(
        kernel,
        out_shape=jax.ShapeDtypeStruct((patches, 2, PATCH, PATCH), F32),
        in_specs=[smem_spec(), vmem_spec()],
        out_specs=vmem_spec(),
        compiler_params=params(),
        cost_estimate=cost(patches * 6, 2 << 20),
        name="wrap_probe",
    )(meta, probe)


def forward(layer, meta, sources, before, right, left, patches):
    wide = patches * PATCH

    def kernel(meta, *refs):
        sources, refs = refs[: -9], refs[-9:]
        before, right, left, trans, after, window, field, half, sems = refs
        fetch(meta, sources, window, sems, patches)
        for p in range(patches):
            for k in range(PATCH // BSIDE):
                tr, ti = patch_rows(meta, window, p, k)
                trans[at_rows(0, k), cols(p)] = tr.astype(BF16)
                trans[at_rows(1, k), cols(p)] = ti.astype(BF16)
                tr = tr + 1.0
                if layer == 0:
                    fr, fi = before[p, 0, rows(k), :], before[p, 1, rows(k), :]
                else:
                    fr = before[at_rows(0, k), cols(p)].astype(F32)
                    fi = before[at_rows(1, k), cols(p)].astype(F32)
                field[at_rows(p, k), cols(0)] = (tr * fr - ti * fi).astype(BF16)
                field[at_rows(p, k), cols(1)] = (tr * fi + ti * fr).astype(BF16)

        def put(c, value):
            after[cols(c), :] = value.astype(BF16)

        propagate(field, half, right, left, patches, put)

    plane = jax.ShapeDtypeStruct((2 * PATCH, wide), BF16)
    return pl.pallas_call(
        kernel,
        out_shape=(plane, plane),
        in_specs=[smem_spec()] + [any_spec()] * len(sources) + [vmem_spec()] * 3,
        out_specs=(vmem_spec(), vmem_spec()),
        scratch_shapes=[
            pltpu.VMEM((patches, WIN, 2, BSIDE, TALL), BF16),
            pltpu.VMEM((wide, 2 * PATCH), BF16),
            pltpu.VMEM((2 * PATCH, wide), BF16),
            pltpu.SemaphoreType.DMA((patches, WIN)),
        ],
        compiler_params=params(),
        cost_estimate=cost(patches * 2, 4 << 20),
        name=f"forward_{layer}",
    )(meta, *sources, before, right, left)


def back_step(meta, p, k, g, q, t, grid, field):
    gr, gi = g
    qr, qi = q
    tr, ti = t
    add_gradient(meta, grid, p, k, (gr * qr + gi * qi, gi * qr - gr * qi))
    field[at_rows(p, k), cols(0)] = (tr * gr + ti * gi).astype(BF16)
    field[at_rows(p, k), cols(1)] = (ti * gr - tr * gi).astype(BF16)


def clear(grid):
    @pl.loop(0, grid.shape[0])
    def _(n):
        grid[n] = jnp.zeros(grid.shape[1:], BF16)


def put_conjugate(out):
    def put(c, value):
        out[cols(c), :] = (-value if c else value).astype(BF16)

    return put


def far_field(meta, sources, before, amplitudes, tabs, pieces, patches):
    wide = patches * PATCH
    n_out = len(pieces)

    def kernel(meta, *refs):
        n_in = len(sources)
        sources_, refs = refs[:n_in], refs[n_in:]
        before, measured, hr, hl, fl, fr = refs[:6]
        outs, refs = refs[6 : 6 + n_out], refs[6 + n_out :]
        after, window, field, half, other, trans, grid, sems, out_sems = refs
        fetch(meta, sources_, window, sems, patches)
        clear(grid)
        for p in range(patches):
            for k in range(PATCH // BSIDE):
                tr, ti = patch_rows(meta, window, p, k)
                trans[at_rows(0, k), cols(p)] = tr.astype(BF16)
                trans[at_rows(1, k), cols(p)] = ti.astype(BF16)
                tr = tr + 1.0
                qr = before[at_rows(0, k), cols(p)].astype(F32)
                qi = before[at_rows(1, k), cols(p)].astype(F32)
                field[at_rows(p, k), cols(0)] = (tr * qr - ti * qi).astype(BF16)
                field[at_rows(p, k), cols(1)] = (tr * qi + ti * qr).astype(BF16)
        for p in range(patches):
            my, mx = shifts(meta, p)
            for c in range(2):
                turned = dot_nt(my, field[cols(p), cols(c)]).astype(BF16)
                half[cols(c), cols(p)] = dot(turned, mx).astype(BF16)
        for c in range(2):
            y = dot(fl[cols(c), :], half[...])
            for p in range(patches):
                other[cols(p), cols(c)] = y[:, p * PATCH : (p + 1) * PATCH].astype(BF16)
        for p in range(patches):
            far = dot(other[cols(p), :], fr[...])
            real, imag = far[:, :PATCH], far[:, PATCH:]
            modulus = jnp.sqrt(real * real + imag * imag)
            keeping = 1.0 - measured[p] / jnp.maximum(modulus, FLOOR)
            half[cols(0), cols(p)] = (real * keeping).astype(BF16)
            half[cols(1), cols(p)] = (-imag * keeping).astype(BF16)
        for c in range(2):
            y = dot(fl[cols(c), :], half[...])
            for p in range(patches):
                other[cols(p), cols(c)] = y[:, p * PATCH : (p + 1) * PATCH].astype(BF16)
        for p in range(patches):
            g = dot(other[cols(p), :], fr[...])
            my, mx = shifts(meta, p)
            for c in range(2):
                part = g[:, c * PATCH : (c + 1) * PATCH]
                part = (-part if c else part).astype(BF16)
                turned = dot_nt(mx, part).astype(BF16)
                half[cols(c), cols(p)] = dot(turned, my).astype(BF16)
        for p in range(patches):
            for k in range(PATCH // BSIDE):
                load = lambda ref, c: ref[at_rows(c, k), cols(p)].astype(F32)
                back_step(
                    meta,
                    p,
                    k,
                    (load(half, 0), load(half, 1)),
                    (load(before, 0), load(before, 1)),
                    (load(trans, 0) + 1.0, load(trans, 1)),
                    grid,
                    field,
                )
        copies = send_out(grid, outs, out_sems)
        propagate(field, half, hr, hl, patches, put_conjugate(after))
        for copy in copies:
            copy.wait()

    plane = jax.ShapeDtypeStruct((2 * PATCH, wide), BF16)
    strips = [jax.ShapeDtypeStruct((n, 2, BSIDE, TALL), BF16) for n in pieces]
    *outs, after = pl.pallas_call(
        kernel,
        out_shape=(*strips, plane),
        in_specs=[smem_spec()] + [any_spec()] * len(sources) + [vmem_spec()] * 6,
        out_specs=(*[any_spec()] * n_out, vmem_spec()),
        scratch_shapes=[
            pltpu.VMEM((patches, WIN, 2, BSIDE, TALL), BF16),
            pltpu.VMEM((wide, 2 * PATCH), BF16),
            pltpu.VMEM((2 * PATCH, wide), BF16),
            pltpu.VMEM((wide, 2 * PATCH), BF16),
            pltpu.VMEM((2 * PATCH, wide), BF16),
            pltpu.VMEM((sum(pieces), 2, BSIDE, TALL), BF16),
            pltpu.SemaphoreType.DMA((patches, WIN)),
            pltpu.SemaphoreType.DMA((n_out,)),
        ],
        compiler_params=params(),
        cost_estimate=cost(patches * 8, 8 << 20),
        name="far_field",
    )(meta, *sources, before, amplitudes, *tabs)
    return outs, after


def backward(layer, meta, adjoint, carried, trans, right, left, pieces, patches):
    wide = patches * PATCH
    n_out = len(pieces)

    def kernel(meta, adjoint, carried, trans, right, left, *refs):
        outs, refs = refs[:n_out], refs[n_out:]
        after, field, half, grid, out_sems = refs
        clear(grid)
        for p in range(patches):
            for k in range(PATCH // BSIDE):
                load = lambda ref, c: ref[at_rows(c, k), cols(p)].astype(F32)
                back_step(
                    meta,
                    p,
                    k,
                    (load(adjoint, 0), load(adjoint, 1)),
                    (load(carried, 0), load(carried, 1)),
                    (load(trans, 0) + 1.0, load(trans, 1)),
                    grid,
                    field,
                )
        copies = send_out(grid, outs, out_sems)
        propagate(field, half, right, left, patches, put_conjugate(after))
        for copy in copies:
            copy.wait()

    plane = jax.ShapeDtypeStruct((2 * PATCH, wide), BF16)
    strips = [jax.ShapeDtypeStruct((n, 2, BSIDE, TALL), BF16) for n in pieces]
    *outs, after = pl.pallas_call(
        kernel,
        out_shape=(*strips, plane),
        in_specs=[smem_spec()] + [vmem_spec()] * 5,
        out_specs=(*[any_spec()] * n_out, vmem_spec()),
        scratch_shapes=[
            pltpu.VMEM((wide, 2 * PATCH), BF16),
            pltpu.VMEM((2 * PATCH, wide), BF16),
            pltpu.VMEM((sum(pieces), 2, BSIDE, TALL), BF16),
            pltpu.SemaphoreType.DMA((n_out,)),
        ],
        compiler_params=params(),
        cost_estimate=cost(patches * 2, 6 << 20),
        name=f"backward_{layer}",
    )(meta, adjoint, carried, trans, right, left)
    return outs, after


def first_slice(meta, adjoint, probe, trans, pieces, patches):
    wide = patches * PATCH
    n_out = len(pieces)

    def kernel(meta, adjoint, probe, trans, *refs):
        outs, refs = refs[:n_out], refs[n_out:]
        total, field, grid, out_sems = refs
        clear(grid)
        for p in range(patches):
            for k in range(PATCH // BSIDE):
                load = lambda ref, c: ref[at_rows(c, k), cols(p)].astype(F32)
                gr, gi = load(adjoint, 0), load(adjoint, 1)
                tr, ti = load(trans, 0) + 1.0, load(trans, 1)
                pr, pi = probe[p, 0, rows(k), :], probe[p, 1, rows(k), :]
                add_gradient(meta, grid, p, k, (gr * pr + gi * pi, gi * pr - gr * pi))
                field[at_rows(p, k), cols(0)] = (gr * tr + gi * ti).astype(BF16)
                field[at_rows(p, k), cols(1)] = (gi * tr - gr * ti).astype(BF16)
        copies = send_out(grid, outs, out_sems)
        moves = [shifts(meta, p) for p in range(patches)]
        for c in range(2):
            terms = [
                dot(dot_nt(my, field[cols(p), cols(c)]).astype(BF16), mx)
                for p, (my, mx) in enumerate(moves)
            ]
            total[c] = sum(terms[1:], terms[0]).astype(BF16)
        for copy in copies:
            copy.wait()

    strips = [jax.ShapeDtypeStruct((n, 2, BSIDE, TALL), BF16) for n in pieces]
    *outs, total = pl.pallas_call(
        kernel,
        out_shape=(*strips, jax.ShapeDtypeStruct((2, PATCH, PATCH), BF16)),
        in_specs=[smem_spec()] + [vmem_spec()] * 3,
        out_specs=(*[any_spec()] * n_out, vmem_spec()),
        scratch_shapes=[
            pltpu.VMEM((wide, 2 * PATCH), BF16),
            pltpu.VMEM((sum(pieces), 2, BSIDE, TALL), BF16),
            pltpu.SemaphoreType.DMA((n_out,)),
        ],
        compiler_params=params(),
        cost_estimate=cost(patches, 6 << 20),
        name="first_slice",
    )(meta, adjoint, probe, trans)
    return outs, total


def lane_group(shape):
    return lax.broadcasted_iota(jnp.int32, shape, 1) // BSIDE


def to_strips(blocks):
    flat = blocks.reshape(-1, BSIDE * BSIDE)

    def kernel(flat, *refs):
        outs, lanes = refs[:-1], refs[-1]
        group = lane_group((8, 128))
        for ag in range(8):
            lanes[ag] = flat[:, ag * 128 : (ag + 1) * 128]
        for s in range(SLICES):
            for t in range(2):
                tall = []
                for ag in range(8):
                    chunk = [
                        lanes[ag, pl.ds(t * 128 + band * 8 + 2 * s + c, 8, stride=16), :]
                        for band in range(2)
                        for c in range(2)
                    ]
                    for a4 in range(4):
                        value = None
                        for n in range(4):
                            move = (n - a4) % 4 * BSIDE
                            moved = pltpu.roll(chunk[n], move, 1) if move else chunk[n]
                            value = moved if n == 0 else jnp.where(group == n, moved, value)
                        tall.append(value)
                for half in range(2):
                    square = jnp.concatenate(tall[half * 16 : half * 16 + 16], axis=0)
                    square = jnp.transpose(square).astype(BF16)
                    for n in range(4):
                        outs[s][n // 2, n % 2, :, pl.ds(t * PATCH + half * 128, 128)] = square[
                            n * BSIDE : (n + 1) * BSIDE
                        ]

    return pl.pallas_call(
        kernel,
        out_shape=[jax.ShapeDtypeStruct((2, 2, BSIDE, TALL), BF16)] * SLICES,
        in_specs=[vmem_spec()],
        out_specs=[vmem_spec()] * SLICES,
        scratch_shapes=[pltpu.VMEM((8, flat.shape[0], 128), F32)],
        compiler_params=params(),
        cost_estimate=pl.CostEstimate(flops=0, bytes_accessed=2 << 20, transcendentals=0),
        name="to_strips",
    )(flat)


def to_blocks(terms):
    counts = [len(term) for term in terms]

    def kernel(*refs):
        out, lanes = refs[-2:]
        group = lane_group((8, 128))
        start = 0
        for s in range(SLICES):
            parts = refs[start : start + counts[s]]
            start += counts[s]
            for t in range(2):
                for half in range(2):
                    pieces = []
                    for n in range(4):
                        spot = (n // 2, n % 2, slice(None), pl.ds(t * PATCH + half * 128, 128))
                        value = parts[0][spot].astype(F32)
                        for part in parts[1:]:
                            value = value + part[spot].astype(F32)
                        pieces.append(value)
                    tall = jnp.transpose(jnp.concatenate(pieces, axis=0))
                    for g in range(4):
                        chunk = [tall[(g * 4 + a4) * 8 : (g * 4 + a4) * 8 + 8] for a4 in range(4)]
                        ag = half * 4 + g
                        for n in range(4):
                            value = None
                            for a4 in range(4):
                                move = (a4 - n) % 4 * BSIDE
                                moved = pltpu.roll(chunk[a4], move, 1) if move else chunk[a4]
                                value = moved if a4 == 0 else jnp.where(group == a4, moved, value)
                            row = t * 128 + n // 2 * 8 + 2 * s + n % 2
                            lanes[ag, pl.ds(row, 8, stride=16), :] = value
        for ag in range(8):
            out[:, ag * 128 : (ag + 1) * 128] = lanes[ag]

    flat = [part for term in terms for part in term]
    out = pl.pallas_call(
        kernel,
        out_shape=jax.ShapeDtypeStruct((FOOT * COL_BANDS * 2 * SLICES, BSIDE * BSIDE), F32),
        in_specs=[vmem_spec()] * len(flat),
        out_specs=vmem_spec(),
        scratch_shapes=[pltpu.VMEM((8, FOOT * COL_BANDS * 2 * SLICES, 128), F32)],
        compiler_params=params(),
        cost_estimate=pl.CostEstimate(flops=0, bytes_accessed=2 << 20, transcendentals=0),
        name="to_blocks",
    )(*flat)
    return out.reshape(FOOT * COL_BANDS, 2 * SLICES, BSIDE * BSIDE)


def work(meta, get_sources, probe, amplitudes, pieces):
    patches = amplitudes.shape[0]
    hr, hl, fl, fr = tables()
    probes = wrap_probe(meta, probe, patches)
    carried, trans = [probes], []
    for layer in range(SLICES - 1):
        t, q = forward(layer, meta, get_sources(layer), carried[-1], hr, hl, patches)
        trans.append(t)
        carried.append(q)
    grads = [None] * SLICES
    grads[-1], adjoint = far_field(
        meta, get_sources(SLICES - 1), carried[-1], amplitudes, (hr, hl, fl, fr), pieces, patches
    )
    for layer in range(SLICES - 2, 0, -1):
        grads[layer], adjoint = backward(
            layer, meta, adjoint, carried[layer], trans[layer], hr, hl, pieces, patches
        )
    grads[0], total = first_slice(meta, adjoint, probes, trans[0], pieces, patches)
    return grads, total


def describe(top, left, source_of, target_of, last):
    first = left // BSIDE
    strips = jnp.minimum(first[:, None] + jnp.arange(WIN, dtype=jnp.int32)[None, :], last)
    columns = [top[:, None], (left % BSIDE)[:, None], source_of(strips), target_of(strips)]
    return jnp.concatenate(columns, axis=1).astype(jnp.int32)


RING = (0, 1, 3, 2)


def ring_place(z):
    return z ^ (z >> 1)


def scan_pairs(move):
    out = []
    for i in range(16):
        z, y, core = i // 4, i // 2 % 2, i % 2
        z, y, core = move(z, y, core)
        out.append((i, z * 4 + y * 2 + core))
    return out


def ring_pairs(steps):
    return scan_pairs(lambda z, y, core: (RING[(RING.index(z) + steps) % 4], y, core))


Y_PAIRS = scan_pairs(lambda z, y, core: (z, 1 - y, core))
CORE_PAIRS = scan_pairs(lambda z, y, core: (z, y, 1 - core))


def send(value, pairs):
    return lax.ppermute(value, "scan", pairs)


def gather_slice(own):
    ring = [own]
    for _ in range(3):
        ring.append(send(ring[-1], ring_pairs(1)))
    line = jnp.concatenate(ring, axis=0)
    line_core = send(line, CORE_PAIRS)
    plane = send(line, Y_PAIRS)
    plane_core = send(plane, CORE_PAIRS)
    return (line, plane, line_core, plane_core)


def widen(value):
    return value.astype(F32)


def scatter_slice(grads):
    here, over_y, over_core = grads
    came = send(over_core, CORE_PAIRS)
    over_y = (widen(over_y) + widen(came[8:])).astype(BF16)
    came_y = send(over_y, Y_PAIRS)
    line = (widen(here) + widen(came[:8]) + widen(came_y)).astype(BF16)
    line = line.reshape(4, COL_BANDS, *line.shape[1:])
    return [line[0]] + [send(line[d], ring_pairs(d)) for d in range(1, 4)]


def sum_probe(total, n_terms):
    core = lax.axis_index("scan") % 2
    mine = jnp.where(core == 0, total[0], total[1])
    theirs = jnp.where(core == 0, total[1], total[0])
    mine = (widen(mine) + widen(send(theirs, CORE_PAIRS))).astype(BF16)
    mine = (widen(mine) + widen(send(mine, Y_PAIRS))).astype(BF16)
    parts = [send(mine, ring_pairs(d)) for d in range(1, 4)]
    mine = sum((widen(part) for part in parts), widen(mine)) / math.sqrt(n_terms)
    other = send(mine, CORE_PAIRS)
    return jnp.where(core == 0, jnp.stack([mine, other]), jnp.stack([other, mine]))


def on_small(object_blocks, probe, positions, anchors, amplitudes):
    me = lax.axis_index("scan")
    z, y, core = me // 4, me // 2 % 2, me % 2
    corner = anchors[0] * BSIDE

    def place(strips, sign):
        owner, band = strips % OWN_COLS, strips // OWN_COLS
        step = (sign * (ring_place(owner // 4) - ring_place(z))) % 4
        over = (owner % 2 ^ core) * 8 + (owner // 2 % 2 ^ y) * 4 + step
        return over * COL_BANDS + band

    meta = describe(
        positions[:, 0] + corner[0],
        positions[:, 1] + corner[1],
        lambda strips: place(strips, -1),
        lambda strips: place(strips, 1),
        OWN_COLS * COL_BANDS - 1,
    )
    own = to_strips(object_blocks)
    sources = [gather_slice(part) for part in own]
    grads, total = work(meta, lambda s: sources[s], probe, amplitudes, (8, 8, 16))
    terms = [scatter_slice(grad) for grad in grads]
    n_terms = lax.axis_size("scan") * positions.shape[0]
    return (to_blocks(terms), sum_probe(total, n_terms))


def footprint_slots(anchor_row, anchor_col, target, slot_number, own_rows):
    per_col = FOOT // OWN_COLS
    first_row = (target // OWN_COLS - anchor_row) % own_rows
    first_col = (target % OWN_COLS - anchor_col) % OWN_COLS
    inner_row = first_row + own_rows * (slot_number // per_col)
    inner_col = first_col + OWN_COLS * (slot_number % per_col)
    row_block = anchor_row + inner_row
    col_block = anchor_col + inner_col
    local = row_block // own_rows * COL_BANDS + col_block // OWN_COLS
    return (inner_row * FOOT + inner_col, local)


def on_any(object_blocks, probe, positions, anchors, amplitudes):
    n_scan = lax.axis_size("scan")
    own_rows = n_scan // OWN_COLS
    capacity = FOOT * FOOT // n_scan
    per_col = FOOT // OWN_COLS
    channels = object_blocks.shape[1]
    anchor_row = anchors[0, 0]
    anchor_col = anchors[0, 1]
    targets = jnp.arange(n_scan, dtype=jnp.int32)[:, None]
    slots = jnp.arange(capacity, dtype=jnp.int32)[None, :]
    send_order, wanted = footprint_slots(anchor_row, anchor_col, targets, slots, own_rows)
    inner = jnp.arange(FOOT, dtype=jnp.int32)
    inner_row = inner[:, None]
    inner_col = inner[None, :]
    holder = (anchor_row + inner_row) % own_rows * OWN_COLS + (anchor_col + inner_col) % OWN_COLS
    arrival = (holder * capacity + inner_row // own_rows * per_col + inner_col // OWN_COLS).reshape(
        -1
    )
    stored = object_blocks.astype(BF16)
    asked = lax.all_to_all(wanted, "scan", split_axis=0, concat_axis=0, tiled=True)
    found = jnp.take(stored, asked, axis=0)
    received = lax.all_to_all(found, "scan", split_axis=0, concat_axis=0, tiled=True)
    footprint = jnp.take(
        received.reshape(n_scan * capacity, channels, BSIDE * BSIDE), arrival, axis=0
    )
    strips = (
        footprint.reshape(2, 8, FOOT, SLICES, 2, BSIDE, BSIDE)
        .transpose(3, 2, 4, 6, 0, 5, 1)
        .reshape(SLICES, FOOT, 2, BSIDE, TALL)
    )
    meta = describe(
        positions[:, 0], positions[:, 1], lambda strips: strips, lambda strips: strips, FOOT - 1
    )
    grads, total = work(meta, lambda s: (strips[s],), probe, amplitudes, (FOOT,))
    blocked = (
        jnp.stack([grad[0] for grad in grads])
        .reshape(SLICES, FOOT, 2, BSIDE, 2, BSIDE, 8)
        .transpose(4, 6, 1, 0, 2, 5, 3)
        .reshape(FOOT * FOOT, channels, BSIDE * BSIDE)
    )
    outgoing = jnp.take(blocked, send_order.reshape(-1), axis=0).reshape(
        n_scan, capacity, channels, BSIDE * BSIDE
    )
    incoming = lax.all_to_all(outgoing, "scan", split_axis=0, concat_axis=0, tiled=True)
    owned = jnp.arange(object_blocks.shape[0], dtype=jnp.int32)
    selector = (asked.reshape(-1)[:, None] == owned[None, :]).astype(F32)
    object_gradient = jnp.einsum(
        "sk,scb->kcb",
        selector,
        incoming.reshape(n_scan * capacity, channels, BSIDE * BSIDE).astype(F32),
        precision=lax.Precision.HIGHEST,
    )
    summed = lax.psum(widen(total), "scan")
    return (object_gradient, summed / math.sqrt(n_scan * positions.shape[0]))


def solution(mesh):
    in_specs = (
        P(("group", "scan"), None, None),
        P("group", None, None),
        P(("group", "scan"), None),
        P(("group", "scan"), None),
        P(("group", "scan"), None, None),
    )
    out_specs = (P(("group", "scan"), None, None), P("group", None, None))
    small = mesh.shape["scan"] == OWN_COLS
    return jax.shard_map(
        on_small if small else on_any,
        mesh=mesh,
        in_specs=in_specs,
        out_specs=out_specs,
        check_vma=False,
    )
```

```python
import math

import jax
import jax.numpy as jnp
import numpy as np
from jax import lax
from jax.experimental import pallas as pl
from jax.experimental.pallas import tpu as pltpu
from jax.sharding import PartitionSpec as P

PATCH = 256
SLICES = 4
BSIDE = 32
FOOT = 16
OWN_COLS = 16
COL_BANDS = 2
FLOOR = 0.25
WIN = 9
TALL = FOOT * BSIDE
VMEM_BYTES = 20 * 1024 * 1024
F32 = jnp.float32
BF16 = jnp.bfloat16


def lane_rows():
    lane = np.arange(PATCH)
    return lane % 8 * BSIDE + lane // 8


def stacked_right(table):
    real, imag = table
    return np.block([[real, imag], [-imag, real]])


def stacked_left(table):
    real, imag = table
    return np.block([[real, -imag], [imag, real]])


def tables():
    counter = np.arange(PATCH)
    turns = counter[:, None] * counter[None, :] % PATCH
    angles = turns.astype(np.float64) * (2.0 * math.pi / PATCH)
    scaled = 1.0 / math.sqrt(PATCH)
    dft = (np.cos(angles) * scaled, -np.sin(angles) * scaled)
    centred = (counter + PATCH // 2) % PATCH - PATCH // 2
    turns = (4 * counter[:, None] * counter[None, :] - centred[None, :] ** 2) % (4 * PATCH)
    angles = turns.astype(np.float64) * (2.0 * math.pi / (4 * PATCH))
    gap = (counter[:, None] - counter[None, :]) % PATCH
    fresnel = ((np.cos(angles).sum(1) / PATCH)[gap], (np.sin(angles).sum(1) / PATCH)[gap])
    order = lane_rows()
    across = tuple(part.T[np.ix_(order, order)] for part in fresnel)
    down = tuple(part.T for part in fresnel)
    wanted = (
        stacked_right(across),
        stacked_left(down),
        stacked_left(dft),
        stacked_right(dft),
    )
    return tuple(jnp.asarray(t.astype(np.float32)).astype(BF16) for t in wanted)


def dot(left, right):
    return jnp.dot(left, right, preferred_element_type=F32)


def dot_nt(left, right):
    return lax.dot_general(left, right, (((1,), (1,)), ((), ())), preferred_element_type=F32)


def row_of_lane(shape):
    lane = lax.broadcasted_iota(jnp.int32, shape, 1)
    return (lane & 7) * BSIDE + (lane >> 3)


def shifts(meta, p, dtype=BF16):
    top, left = meta[p, 0], meta[p, 1]
    shape = (PATCH, PATCH)
    i = lax.broadcasted_iota(jnp.int32, shape, 0)
    j = lax.broadcasted_iota(jnp.int32, shape, 1)
    my = jnp.where(row_of_lane(shape) == ((i + top) & (PATCH - 1)), 1.0, 0.0).astype(dtype)
    mx = jnp.where(i == ((j + left) & (PATCH - 1)), 1.0, 0.0).astype(dtype)
    return my, mx


def cols(c):
    return pl.ds(c * PATCH, PATCH)


def fetch(meta, sources, window, sems, patches):
    per = sources[0].shape[0]

    def copy(source, place, p, k):
        return pltpu.make_async_copy(source.at[place], window.at[p, k], sems.at[p, k])

    for p in range(patches):
        for k in range(WIN):
            place = meta[p, 2 + k]
            for n, source in enumerate(sources):

                @pl.when(place // per == n)
                def _(source=source, place=place, n=n, p=p, k=k):
                    copy(source, place - n * per, p, k).start()

    for p in range(patches):
        for k in range(WIN):
            copy(sources[0], 0, p, k).wait()


def patch_rows(meta, window, p, k):
    top, left = meta[p, 0], meta[p, 1]
    low = row_of_lane((BSIDE, PATCH)) < top
    out = []
    for c in range(2):

        def pick(slot):
            strip = window[p, slot, c].astype(F32)
            return jnp.where(low, strip[:, PATCH:], strip[:, :PATCH])

        value = pick(k)
        if k == 0:
            b = lax.broadcasted_iota(jnp.int32, (BSIDE, PATCH), 0)
            value = jnp.where(b < left, pick(WIN - 1), value)
        out.append(value)
    return out


def propagate(field, half, right, left, patches, put):
    for p in range(patches):
        y = dot(field[cols(p), :], right[...])
        for c in range(2):
            half[cols(c), cols(p)] = y[:, c * PATCH : (c + 1) * PATCH].astype(BF16)
    for c in range(2):
        put(c, dot(left[cols(c), :], half[...]))


def add_gradient(meta, grid, p, k, pair):
    top, left = meta[p, 0], meta[p, 1]
    low = row_of_lane((BSIDE, PATCH)) < top
    b = lax.broadcasted_iota(jnp.int32, (BSIDE, PATCH), 0)

    def put(slot, c, value):
        place = meta[p, 2 + WIN + slot]
        for half in range(2):
            piece = jnp.where(low if half else jnp.logical_not(low), value, 0.0)
            spot = (place, c, slice(None), slice(half * PATCH, (half + 1) * PATCH))
            if p > 0 or slot == WIN - 1:
                piece = piece + grid[spot].astype(F32)
            grid[spot] = piece.astype(BF16)

    if k > 0:
        for c in range(2):
            put(k, c, pair[c])
        return
    for c in range(2):
        put(0, c, jnp.where(b < left, 0.0, pair[c]))

    @pl.when(left > 0)
    def _():
        for c in range(2):
            put(WIN - 1, c, jnp.where(b < left, pair[c], 0.0))


def send_out(grid, outs, sems):
    start = 0
    copies = []
    for n, out in enumerate(outs):
        size = out.shape[0]
        copies.append(pltpu.make_async_copy(grid.at[pl.ds(start, size)], out, sems.at[n]))
        start += size
    for copy in copies:
        copy.start()
    return copies


def rows(k):
    return pl.ds(k * BSIDE, BSIDE)


def at_rows(c, k):
    return pl.ds(c * PATCH + k * BSIDE, BSIDE)


def any_spec():
    return pl.BlockSpec(memory_space=pl.ANY)


def vmem_spec():
    return pl.BlockSpec(memory_space=pltpu.VMEM)


def smem_spec():
    return pl.BlockSpec(memory_space=pltpu.SMEM)


def params():
    return pltpu.CompilerParams(vmem_limit_bytes=VMEM_BYTES)


def cost(microseconds):
    return pl.CostEstimate(flops=0, bytes_accessed=int(microseconds * 3.6e6), transcendentals=0)


def wrap_probe(meta, probe, patches):
    def kernel(meta, probe, out):
        for p in range(patches):
            my, mx = shifts(meta, p, F32)
            for c in range(2):
                half = lax.dot_general(
                    mx,
                    probe[c],
                    (((1,), (1,)), ((), ())),
                    precision=lax.Precision.HIGHEST,
                    preferred_element_type=F32,
                )
                out[p, c] = jnp.dot(
                    half, my, precision=lax.Precision.HIGHEST, preferred_element_type=F32
                )

    return pl.pallas_call(
        kernel,
        out_shape=jax.ShapeDtypeStruct((patches, 2, PATCH, PATCH), F32),
        in_specs=[smem_spec(), vmem_spec()],
        out_specs=vmem_spec(),
        compiler_params=params(),
        cost_estimate=cost(3.3),
        name="wrap_probe",
    )(meta, probe)


def forward(layer, meta, sources, before, right, left, patches):
    wide = patches * PATCH

    def kernel(meta, *refs):
        sources, refs = refs[: -9], refs[-9:]
        before, right, left, trans, after, window, field, half, sems = refs
        fetch(meta, sources, window, sems, patches)
        for p in range(patches):
            for k in range(PATCH // BSIDE):
                tr, ti = patch_rows(meta, window, p, k)
                trans[at_rows(0, k), cols(p)] = tr.astype(BF16)
                trans[at_rows(1, k), cols(p)] = ti.astype(BF16)
                tr = tr + 1.0
                if layer == 0:
                    fr, fi = before[p, 0, rows(k), :], before[p, 1, rows(k), :]
                else:
                    fr = before[at_rows(0, k), cols(p)].astype(F32)
                    fi = before[at_rows(1, k), cols(p)].astype(F32)
                field[at_rows(p, k), cols(0)] = (tr * fr - ti * fi).astype(BF16)
                field[at_rows(p, k), cols(1)] = (tr * fi + ti * fr).astype(BF16)

        def put(c, value):
            after[cols(c), :] = value.astype(BF16)

        propagate(field, half, right, left, patches, put)

    plane = jax.ShapeDtypeStruct((2 * PATCH, wide), BF16)
    return pl.pallas_call(
        kernel,
        out_shape=(plane, plane),
        in_specs=[smem_spec()] + [any_spec()] * len(sources) + [vmem_spec()] * 3,
        out_specs=(vmem_spec(), vmem_spec()),
        scratch_shapes=[
            pltpu.VMEM((patches, WIN, 2, BSIDE, TALL), BF16),
            pltpu.VMEM((wide, 2 * PATCH), BF16),
            pltpu.VMEM((2 * PATCH, wide), BF16),
            pltpu.SemaphoreType.DMA((patches, WIN)),
        ],
        compiler_params=params(),
        cost_estimate=cost(3.5),
        name=f"forward_{layer}",
    )(meta, *sources, before, right, left)


def back_step(meta, p, k, g, q, t, grid, field):
    gr, gi = g
    qr, qi = q
    tr, ti = t
    add_gradient(meta, grid, p, k, (gr * qr + gi * qi, gi * qr - gr * qi))
    field[at_rows(p, k), cols(0)] = (tr * gr + ti * gi).astype(BF16)
    field[at_rows(p, k), cols(1)] = (ti * gr - tr * gi).astype(BF16)


def clear(grid):
    @pl.loop(0, grid.shape[0])
    def _(n):
        grid[n] = jnp.zeros(grid.shape[1:], BF16)


def put_conjugate(out):
    def put(c, value):
        out[cols(c), :] = (-value if c else value).astype(BF16)

    return put


def far_field(meta, sources, before, amplitudes, tabs, pieces, patches):
    wide = patches * PATCH
    n_out = len(pieces)

    def kernel(meta, *refs):
        n_in = len(sources)
        sources_, refs = refs[:n_in], refs[n_in:]
        before, measured, hr, hl, fl, fr = refs[:6]
        outs, refs = refs[6 : 6 + n_out], refs[6 + n_out :]
        after, window, field, half, other, trans, grid, sems, out_sems = refs
        fetch(meta, sources_, window, sems, patches)
        clear(grid)
        for p in range(patches):
            for k in range(PATCH // BSIDE):
                tr, ti = patch_rows(meta, window, p, k)
                trans[at_rows(0, k), cols(p)] = tr.astype(BF16)
                trans[at_rows(1, k), cols(p)] = ti.astype(BF16)
                tr = tr + 1.0
                qr = before[at_rows(0, k), cols(p)].astype(F32)
                qi = before[at_rows(1, k), cols(p)].astype(F32)
                field[at_rows(p, k), cols(0)] = (tr * qr - ti * qi).astype(BF16)
                field[at_rows(p, k), cols(1)] = (tr * qi + ti * qr).astype(BF16)
        for p in range(patches):
            my, mx = shifts(meta, p)
            for c in range(2):
                turned = dot_nt(my, field[cols(p), cols(c)]).astype(BF16)
                half[cols(c), cols(p)] = dot(turned, mx).astype(BF16)
        for c in range(2):
            y = dot(fl[cols(c), :], half[...])
            for p in range(patches):
                other[cols(p), cols(c)] = y[:, p * PATCH : (p + 1) * PATCH].astype(BF16)
        for p in range(patches):
            far = dot(other[cols(p), :], fr[...])
            real, imag = far[:, :PATCH], far[:, PATCH:]
            modulus = jnp.sqrt(real * real + imag * imag)
            keeping = 1.0 - measured[p] / jnp.maximum(modulus, FLOOR)
            half[cols(0), cols(p)] = (real * keeping).astype(BF16)
            half[cols(1), cols(p)] = (-imag * keeping).astype(BF16)
        for c in range(2):
            y = dot(fl[cols(c), :], half[...])
            for p in range(patches):
                other[cols(p), cols(c)] = y[:, p * PATCH : (p + 1) * PATCH].astype(BF16)
        for p in range(patches):
            g = dot(other[cols(p), :], fr[...])
            my, mx = shifts(meta, p)
            for c in range(2):
                part = g[:, c * PATCH : (c + 1) * PATCH]
                part = (-part if c else part).astype(BF16)
                turned = dot_nt(mx, part).astype(BF16)
                half[cols(c), cols(p)] = dot(turned, my).astype(BF16)
        for p in range(patches):
            for k in range(PATCH // BSIDE):
                load = lambda ref, c: ref[at_rows(c, k), cols(p)].astype(F32)
                back_step(
                    meta,
                    p,
                    k,
                    (load(half, 0), load(half, 1)),
                    (load(before, 0), load(before, 1)),
                    (load(trans, 0) + 1.0, load(trans, 1)),
                    grid,
                    field,
                )
        copies = send_out(grid, outs, out_sems)
        propagate(field, half, hr, hl, patches, put_conjugate(after))
        for copy in copies:
            copy.wait()

    plane = jax.ShapeDtypeStruct((2 * PATCH, wide), BF16)
    strips = [jax.ShapeDtypeStruct((n, 2, BSIDE, TALL), BF16) for n in pieces]
    *outs, after = pl.pallas_call(
        kernel,
        out_shape=(*strips, plane),
        in_specs=[smem_spec()] + [any_spec()] * len(sources) + [vmem_spec()] * 6,
        out_specs=(*[any_spec()] * n_out, vmem_spec()),
        scratch_shapes=[
            pltpu.VMEM((patches, WIN, 2, BSIDE, TALL), BF16),
            pltpu.VMEM((wide, 2 * PATCH), BF16),
            pltpu.VMEM((2 * PATCH, wide), BF16),
            pltpu.VMEM((wide, 2 * PATCH), BF16),
            pltpu.VMEM((2 * PATCH, wide), BF16),
            pltpu.VMEM((sum(pieces), 2, BSIDE, TALL), BF16),
            pltpu.SemaphoreType.DMA((patches, WIN)),
            pltpu.SemaphoreType.DMA((n_out,)),
        ],
        compiler_params=params(),
        cost_estimate=cost(7.5),
        name="far_field",
    )(meta, *sources, before, amplitudes, *tabs)
    return outs, after


def backward(layer, meta, adjoint, carried, trans, right, left, pieces, patches):
    wide = patches * PATCH
    n_out = len(pieces)

    def kernel(meta, adjoint, carried, trans, right, left, *refs):
        outs, refs = refs[:n_out], refs[n_out:]
        after, field, half, grid, out_sems = refs
        clear(grid)
        for p in range(patches):
            for k in range(PATCH // BSIDE):
                load = lambda ref, c: ref[at_rows(c, k), cols(p)].astype(F32)
                back_step(
                    meta,
                    p,
                    k,
                    (load(adjoint, 0), load(adjoint, 1)),
                    (load(carried, 0), load(carried, 1)),
                    (load(trans, 0) + 1.0, load(trans, 1)),
                    grid,
                    field,
                )
        copies = send_out(grid, outs, out_sems)
        propagate(field, half, right, left, patches, put_conjugate(after))
        for copy in copies:
            copy.wait()

    plane = jax.ShapeDtypeStruct((2 * PATCH, wide), BF16)
    strips = [jax.ShapeDtypeStruct((n, 2, BSIDE, TALL), BF16) for n in pieces]
    *outs, after = pl.pallas_call(
        kernel,
        out_shape=(*strips, plane),
        in_specs=[smem_spec()] + [vmem_spec()] * 5,
        out_specs=(*[any_spec()] * n_out, vmem_spec()),
        scratch_shapes=[
            pltpu.VMEM((wide, 2 * PATCH), BF16),
            pltpu.VMEM((2 * PATCH, wide), BF16),
            pltpu.VMEM((sum(pieces), 2, BSIDE, TALL), BF16),
            pltpu.SemaphoreType.DMA((n_out,)),
        ],
        compiler_params=params(),
        cost_estimate=cost(2.3),
        name=f"backward_{layer}",
    )(meta, adjoint, carried, trans, right, left)
    return outs, after


def first_slice(meta, adjoint, probe, trans, pieces, patches):
    wide = patches * PATCH
    n_out = len(pieces)

    def kernel(meta, adjoint, probe, trans, *refs):
        outs, refs = refs[:n_out], refs[n_out:]
        total, field, grid, out_sems = refs
        clear(grid)
        for p in range(patches):
            for k in range(PATCH // BSIDE):
                load = lambda ref, c: ref[at_rows(c, k), cols(p)].astype(F32)
                gr, gi = load(adjoint, 0), load(adjoint, 1)
                tr, ti = load(trans, 0) + 1.0, load(trans, 1)
                pr, pi = probe[p, 0, rows(k), :], probe[p, 1, rows(k), :]
                add_gradient(meta, grid, p, k, (gr * pr + gi * pi, gi * pr - gr * pi))
                field[at_rows(p, k), cols(0)] = (gr * tr + gi * ti).astype(BF16)
                field[at_rows(p, k), cols(1)] = (gi * tr - gr * ti).astype(BF16)
        copies = send_out(grid, outs, out_sems)
        moves = [shifts(meta, p) for p in range(patches)]
        for c in range(2):
            terms = [
                dot(dot_nt(my, field[cols(p), cols(c)]).astype(BF16), mx)
                for p, (my, mx) in enumerate(moves)
            ]
            total[c] = sum(terms[1:], terms[0]).astype(BF16)
        for copy in copies:
            copy.wait()

    strips = [jax.ShapeDtypeStruct((n, 2, BSIDE, TALL), BF16) for n in pieces]
    *outs, total = pl.pallas_call(
        kernel,
        out_shape=(*strips, jax.ShapeDtypeStruct((2, PATCH, PATCH), BF16)),
        in_specs=[smem_spec()] + [vmem_spec()] * 3,
        out_specs=(*[any_spec()] * n_out, vmem_spec()),
        scratch_shapes=[
            pltpu.VMEM((wide, 2 * PATCH), BF16),
            pltpu.VMEM((sum(pieces), 2, BSIDE, TALL), BF16),
            pltpu.SemaphoreType.DMA((n_out,)),
        ],
        compiler_params=params(),
        cost_estimate=cost(2.3),
        name="first_slice",
    )(meta, adjoint, probe, trans)
    return outs, total


def lane_group(shape):
    return lax.broadcasted_iota(jnp.int32, shape, 1) // BSIDE


def to_strips(blocks):
    flat = blocks.reshape(-1, BSIDE * BSIDE)

    def kernel(flat, *refs):
        outs, lanes = refs[:-1], refs[-1]
        group = lane_group((8, 128))
        for ag in range(8):
            lanes[ag] = flat[:, ag * 128 : (ag + 1) * 128]
        for s in range(SLICES):
            for t in range(2):
                tall = []
                for ag in range(8):
                    chunk = [
                        lanes[ag, pl.ds(t * 128 + band * 8 + 2 * s + c, 8, stride=16), :]
                        for band in range(2)
                        for c in range(2)
                    ]
                    for a4 in range(4):
                        value = None
                        for n in range(4):
                            move = (n - a4) % 4 * BSIDE
                            moved = pltpu.roll(chunk[n], move, 1) if move else chunk[n]
                            value = moved if n == 0 else jnp.where(group == n, moved, value)
                        tall.append(value)
                for half in range(2):
                    square = jnp.concatenate(tall[half * 16 : half * 16 + 16], axis=0)
                    square = jnp.transpose(square).astype(BF16)
                    for n in range(4):
                        outs[s][n // 2, n % 2, :, pl.ds(t * PATCH + half * 128, 128)] = square[
                            n * BSIDE : (n + 1) * BSIDE
                        ]

    return pl.pallas_call(
        kernel,
        out_shape=[jax.ShapeDtypeStruct((2, 2, BSIDE, TALL), BF16)] * SLICES,
        in_specs=[vmem_spec()],
        out_specs=[vmem_spec()] * SLICES,
        scratch_shapes=[pltpu.VMEM((8, flat.shape[0], 128), F32)],
        compiler_params=params(),
        cost_estimate=cost(1.5),
        name="to_strips",
    )(flat)


def to_blocks(terms):
    counts = [len(term) for term in terms]

    def kernel(*refs):
        out, lanes = refs[-2:]
        group = lane_group((8, 128))
        start = 0
        for s in range(SLICES):
            parts = refs[start : start + counts[s]]
            start += counts[s]
            for t in range(2):
                for half in range(2):
                    pieces = []
                    for n in range(4):
                        spot = (n // 2, n % 2, slice(None), pl.ds(t * PATCH + half * 128, 128))
                        value = parts[0][spot].astype(F32)
                        for part in parts[1:]:
                            value = value + part[spot].astype(F32)
                        pieces.append(value)
                    tall = jnp.transpose(jnp.concatenate(pieces, axis=0))
                    for g in range(4):
                        chunk = [tall[(g * 4 + a4) * 8 : (g * 4 + a4) * 8 + 8] for a4 in range(4)]
                        ag = half * 4 + g
                        for n in range(4):
                            value = None
                            for a4 in range(4):
                                move = (a4 - n) % 4 * BSIDE
                                moved = pltpu.roll(chunk[a4], move, 1) if move else chunk[a4]
                                value = moved if a4 == 0 else jnp.where(group == a4, moved, value)
                            row = t * 128 + n // 2 * 8 + 2 * s + n % 2
                            lanes[ag, pl.ds(row, 8, stride=16), :] = value
        for ag in range(8):
            out[:, ag * 128 : (ag + 1) * 128] = lanes[ag]

    flat = [part for term in terms for part in term]
    out = pl.pallas_call(
        kernel,
        out_shape=jax.ShapeDtypeStruct((FOOT * COL_BANDS * 2 * SLICES, BSIDE * BSIDE), F32),
        in_specs=[vmem_spec()] * len(flat),
        out_specs=vmem_spec(),
        scratch_shapes=[pltpu.VMEM((8, FOOT * COL_BANDS * 2 * SLICES, 128), F32)],
        compiler_params=params(),
        cost_estimate=cost(1.5),
        name="to_blocks",
    )(*flat)
    return out.reshape(FOOT * COL_BANDS, 2 * SLICES, BSIDE * BSIDE)


def after(value, *events):
    return lax.optimization_barrier((value, *events))[0]


def describe(top, left, source_of, target_of, last):
    first = left // BSIDE
    strips = jnp.minimum(first[:, None] + jnp.arange(WIN, dtype=jnp.int32)[None, :], last)
    columns = [top[:, None], (left % BSIDE)[:, None], source_of(strips), target_of(strips)]
    return jnp.concatenate(columns, axis=1).astype(jnp.int32)


FAR, NEAR, OVER_Y, OVER_CORE = 8, 4, 2, 1


def swap(value, bit):
    return lax.ppermute(value, "scan", [(i, i ^ bit) for i in range(16)])


def join(*values):
    return jnp.concatenate(values, axis=0)


def widen(value):
    return value.astype(F32)


def plus(value, *others):
    return sum((widen(other) for other in others), widen(value)).astype(BF16)


def slots(owner, order):
    bits = [(owner & bit) // bit * 2**n for n, bit in enumerate(order)]
    return sum(bits[1:], bits[0])


LINE_FIRST = (FAR, NEAR, OVER_Y, OVER_CORE)
PLANE_FIRST = (OVER_Y, FAR, NEAR, OVER_CORE)


def sum_probe(total, n_terms, events):
    me = lax.axis_index("scan")
    core, y = me % 2, me // 2 % 2
    mine = jnp.where(core == 0, total[0], total[1])
    theirs = jnp.where(core == 0, total[1], total[0])
    mine = plus(mine, swap(after(theirs, events[0]), OVER_CORE))
    mine = mine.reshape(2, PATCH // 2, PATCH)
    theirs = jnp.where(y == 0, mine[1], mine[0])
    mine = jnp.where(y == 0, mine[0], mine[1])
    mine = plus(mine, swap(after(theirs, events[1]), OVER_Y))
    mine = plus(mine, swap(after(mine, events[2]), NEAR))
    mine = (widen(mine) + widen(swap(after(mine, events[3]), FAR))) / math.sqrt(n_terms)
    other = swap(after(mine, events[4]), OVER_Y)
    mine = jnp.where(y == 0, join(mine, other), join(other, mine))
    other = swap(after(mine, events[5]), OVER_CORE)
    return jnp.where(core == 0, jnp.stack([mine, other]), jnp.stack([other, mine]))


def on_small(object_blocks, probe, positions, anchors, amplitudes):
    me = lax.axis_index("scan")
    corner = anchors[0] * BSIDE
    patches = positions.shape[0]

    def described(order):
        def place(strips):
            return slots(strips % OWN_COLS ^ me, order) * COL_BANDS + strips // OWN_COLS

        return describe(
            positions[:, 0] + corner[0],
            positions[:, 1] + corner[1],
            place,
            place,
            OWN_COLS * COL_BANDS - 1,
        )

    meta, meta_last = described(LINE_FIRST), described(PLANE_FIRST)
    hr, hl, fl, fr = tables()
    probes = wrap_probe(meta, probe, patches)
    own = to_strips(object_blocks)

    far0 = swap(own[0], FAR)
    y0a = swap(own[0], OVER_Y)
    y3 = swap(own[3], OVER_Y)
    far1 = swap(after(own[1], far0), FAR)
    near0 = swap(after(join(own[0], far0), probes), NEAR)
    y0b = swap(after(far0, y0a, y3), OVER_Y)
    far2 = swap(after(own[2], far0), FAR)
    near1 = swap(after(join(own[1], far1), near0), NEAR)
    y0c = swap(after(near0, y0b, far1), OVER_Y)
    pair3 = join(own[3], y3)
    far3 = swap(after(pair3, far1), FAR)
    here1 = join(own[1], far1, near1)
    y1 = swap(after(here1, y0c, far2), OVER_Y)
    here0 = join(own[0], far0, near0, y0a, y0b, y0c)
    core0 = swap(after(here0, near1, far2), OVER_CORE)
    trans0, q1 = forward(0, meta, (here0, core0), probes, hr, hl, patches)
    near2 = swap(after(join(own[2], far2), near1, q1), NEAR)
    here2 = join(own[2], far2, near2)
    here3 = join(pair3, far3)
    near3 = swap(after(here3, near2), NEAR)
    y2 = swap(after(here2, q1, y1, far3), OVER_Y)
    here1 = join(here1, y1)
    core1 = swap(after(here1, near2, far3, q1), OVER_CORE)
    trans1, q2 = forward(1, meta, (here1, core1), q1, hr, hl, patches)
    core3a = swap(after(here3, q2), OVER_CORE)
    here2 = join(here2, y2)
    core2 = swap(after(here2, core3a, near3), OVER_CORE)
    trans2, q3 = forward(2, meta, (here2, core2), q2, hr, hl, patches)
    core3b = swap(near3, OVER_CORE)

    pieces = (8, 8, 16)
    (here3, near3, core3), g2 = far_field(
        meta_last,
        (here3, near3, core3a, core3b),
        q3,
        amplitudes,
        (hr, hl, fl, fr),
        pieces,
        patches,
    )

    came3 = swap(core3, OVER_CORE)
    (here2, y2, core2), g1 = backward(2, meta, g2, q2, trans2, hr, hl, pieces, patches)
    came2 = swap(core2, OVER_CORE)
    near3 = swap(after(plus(near3, came3[8:]), g1), NEAR)
    (here1, y1, core1), g0 = backward(1, meta, after(g1, came3), q1, trans1, hr, hl, pieces, patches)
    came1 = swap(core1, OVER_CORE)
    y2 = after(plus(y2, came2[8:]), g0)
    (here0, y0, core0), total = first_slice(
        meta, after(g0, y2), probes, trans0, pieces, patches
    )
    y2 = swap(y2, OVER_Y)
    came0 = swap(core0, OVER_CORE)
    y1 = plus(y1, came1[8:])
    y0 = plus(y0, came0[8:])
    line3 = plus(here3, came3[:8], near3)
    far3 = swap(after(line3[4:], y1, y0), FAR)
    y1 = swap(after(y1, total, y2), OVER_Y)
    line2 = plus(here2, came2[:8], y2)
    near2 = swap(line2[4:], NEAR)
    y0 = swap(after(y0, y1), OVER_Y)
    pair3 = plus(line3[:4], after(far3, y1))
    y3 = swap(pair3[2:], OVER_Y)
    line2 = plus(line2[:4], after(near2, y1))
    far2 = swap(line2[2:], FAR)
    line1 = plus(here1, came1[:8], y1)
    near1 = swap(line1[4:], NEAR)
    line1 = plus(line1[:4], after(near1, y0))
    far1 = swap(line1[2:], FAR)
    line0 = plus(here0, came0[:8], y0)
    near0 = swap(line0[4:], NEAR)
    line0 = plus(line0[:4], near0)
    far0 = swap(line0[2:], FAR)
    probe_gradient = sum_probe(
        total, lax.axis_size("scan") * patches, (y2, y1, y1, y3, y0, near0)
    )
    far0 = after(far0, probe_gradient)
    terms = [(line0[:2], far0), (line1[:2], far1), (line2[:2], far2), (pair3[:2], y3)]
    return (to_blocks(terms), probe_gradient)


def footprint_slots(anchor_row, anchor_col, target, slot_number, own_rows):
    per_col = FOOT // OWN_COLS
    first_row = (target // OWN_COLS - anchor_row) % own_rows
    first_col = (target % OWN_COLS - anchor_col) % OWN_COLS
    inner_row = first_row + own_rows * (slot_number // per_col)
    inner_col = first_col + OWN_COLS * (slot_number % per_col)
    row_block = anchor_row + inner_row
    col_block = anchor_col + inner_col
    local = row_block // own_rows * COL_BANDS + col_block // OWN_COLS
    return (inner_row * FOOT + inner_col, local)


def work(meta, sources, probe, amplitudes, pieces):
    patches = amplitudes.shape[0]
    hr, hl, fl, fr = tables()
    probes = wrap_probe(meta, probe, patches)
    carried, trans = [probes], []
    for layer in range(SLICES - 1):
        t, q = forward(layer, meta, sources[layer], carried[-1], hr, hl, patches)
        trans.append(t)
        carried.append(q)
    grads = [None] * SLICES
    grads[-1], adjoint = far_field(
        meta, sources[-1], carried[-1], amplitudes, (hr, hl, fl, fr), pieces, patches
    )
    for layer in range(SLICES - 2, 0, -1):
        grads[layer], adjoint = backward(
            layer, meta, adjoint, carried[layer], trans[layer], hr, hl, pieces, patches
        )
    grads[0], total = first_slice(meta, adjoint, probes, trans[0], pieces, patches)
    return grads, total


def on_any(object_blocks, probe, positions, anchors, amplitudes):
    n_scan = lax.axis_size("scan")
    own_rows = n_scan // OWN_COLS
    capacity = FOOT * FOOT // n_scan
    per_col = FOOT // OWN_COLS
    channels = object_blocks.shape[1]
    anchor_row = anchors[0, 0]
    anchor_col = anchors[0, 1]
    targets = jnp.arange(n_scan, dtype=jnp.int32)[:, None]
    slots = jnp.arange(capacity, dtype=jnp.int32)[None, :]
    send_order, wanted = footprint_slots(anchor_row, anchor_col, targets, slots, own_rows)
    inner = jnp.arange(FOOT, dtype=jnp.int32)
    inner_row = inner[:, None]
    inner_col = inner[None, :]
    holder = (anchor_row + inner_row) % own_rows * OWN_COLS + (anchor_col + inner_col) % OWN_COLS
    arrival = (holder * capacity + inner_row // own_rows * per_col + inner_col // OWN_COLS).reshape(
        -1
    )
    stored = object_blocks.astype(BF16)
    asked = lax.all_to_all(wanted, "scan", split_axis=0, concat_axis=0, tiled=True)
    found = jnp.take(stored, asked, axis=0)
    received = lax.all_to_all(found, "scan", split_axis=0, concat_axis=0, tiled=True)
    footprint = jnp.take(
        received.reshape(n_scan * capacity, channels, BSIDE * BSIDE), arrival, axis=0
    )
    strips = (
        footprint.reshape(2, 8, FOOT, SLICES, 2, BSIDE, BSIDE)
        .transpose(3, 2, 4, 6, 0, 5, 1)
        .reshape(SLICES, FOOT, 2, BSIDE, TALL)
    )
    meta = describe(
        positions[:, 0], positions[:, 1], lambda strips: strips, lambda strips: strips, FOOT - 1
    )
    sources = [(strips[s],) for s in range(SLICES)]
    grads, total = work(meta, sources, probe, amplitudes, (FOOT,))
    blocked = (
        jnp.stack([grad[0] for grad in grads])
        .reshape(SLICES, FOOT, 2, BSIDE, 2, BSIDE, 8)
        .transpose(4, 6, 1, 0, 2, 5, 3)
        .reshape(FOOT * FOOT, channels, BSIDE * BSIDE)
    )
    outgoing = jnp.take(blocked, send_order.reshape(-1), axis=0).reshape(
        n_scan, capacity, channels, BSIDE * BSIDE
    )
    incoming = lax.all_to_all(outgoing, "scan", split_axis=0, concat_axis=0, tiled=True)
    owned = jnp.arange(object_blocks.shape[0], dtype=jnp.int32)
    selector = (asked.reshape(-1)[:, None] == owned[None, :]).astype(F32)
    object_gradient = jnp.einsum(
        "sk,scb->kcb",
        selector,
        incoming.reshape(n_scan * capacity, channels, BSIDE * BSIDE).astype(F32),
        precision=lax.Precision.HIGHEST,
    )
    summed = lax.psum(widen(total), "scan")
    return (object_gradient, summed / math.sqrt(n_scan * positions.shape[0]))


def solution(mesh):
    in_specs = (
        P(("group", "scan"), None, None),
        P("group", None, None),
        P(("group", "scan"), None),
        P(("group", "scan"), None),
        P(("group", "scan"), None, None),
    )
    out_specs = (P(("group", "scan"), None, None), P("group", None, None))
    small = mesh.shape["scan"] == OWN_COLS
    return jax.shard_map(
        on_small if small else on_any,
        mesh=mesh,
        in_specs=in_specs,
        out_specs=out_specs,
        check_vma=False,
    )
```

```python
import math

import jax
import jax.numpy as jnp
import numpy as np
from jax import lax
from jax.experimental import pallas as pl
from jax.experimental.pallas import tpu as pltpu
from jax.sharding import PartitionSpec as P

PATCH = 256
SLICES = 4
BSIDE = 32
FOOT = 16
OWN_COLS = 16
COL_BANDS = 2
FLOOR = 0.25
WIN = 9
TALL = FOOT * BSIDE
VMEM_BYTES = 16 * 1024 * 1024
SCALE = 3.6e6
F32 = jnp.float32
BF16 = jnp.bfloat16


def lane_rows():
    lane = np.arange(PATCH)
    return lane % 8 * BSIDE + lane // 8


def stacked_right(table):
    real, imag = table
    return np.block([[real, imag], [-imag, real]])


def stacked_left(table):
    real, imag = table
    return np.block([[real, -imag], [imag, real]])


def tables():
    counter = np.arange(PATCH)
    turns = counter[:, None] * counter[None, :] % PATCH
    angles = turns.astype(np.float64) * (2.0 * math.pi / PATCH)
    scaled = 1.0 / math.sqrt(PATCH)
    dft = (np.cos(angles) * scaled, -np.sin(angles) * scaled)
    centred = (counter + PATCH // 2) % PATCH - PATCH // 2
    turns = (4 * counter[:, None] * counter[None, :] - centred[None, :] ** 2) % (4 * PATCH)
    angles = turns.astype(np.float64) * (2.0 * math.pi / (4 * PATCH))
    gap = (counter[:, None] - counter[None, :]) % PATCH
    fresnel = ((np.cos(angles).sum(1) / PATCH)[gap], (np.sin(angles).sum(1) / PATCH)[gap])
    order = lane_rows()
    across = tuple(part.T[np.ix_(order, order)] for part in fresnel)
    down = tuple(part.T for part in fresnel)
    wanted = (
        stacked_right(across),
        stacked_left(down),
        stacked_left(dft),
        stacked_right(dft),
    )
    return tuple(jnp.asarray(t.astype(np.float32)).astype(BF16) for t in wanted)


def dot(left, right):
    return jnp.dot(left, right, preferred_element_type=F32)


def dot_nt(left, right):
    return lax.dot_general(left, right, (((1,), (1,)), ((), ())), preferred_element_type=F32)


def row_of_lane(shape):
    lane = lax.broadcasted_iota(jnp.int32, shape, 1)
    return (lane & 7) * BSIDE + (lane >> 3)


def shifts(meta, p, dtype=BF16):
    top, left = meta[p, 0], meta[p, 1]
    shape = (PATCH, PATCH)
    i = lax.broadcasted_iota(jnp.int32, shape, 0)
    j = lax.broadcasted_iota(jnp.int32, shape, 1)
    my = jnp.where(row_of_lane(shape) == ((i + top) & (PATCH - 1)), 1.0, 0.0).astype(dtype)
    mx = jnp.where(i == ((j + left) & (PATCH - 1)), 1.0, 0.0).astype(dtype)
    return my, mx


def cols(c):
    return pl.ds(c * PATCH, PATCH)


def strip_copy(source, place, window, sems, p, k):
    return pltpu.make_async_copy(source.at[place], window.at[p, k], sems.at[p, k])


def fetch(meta, sources, window, sems, patches):
    per = sources[0].shape[0]
    for p in range(patches):
        for k in range(WIN):
            place = meta[p, 2 + k]
            for m, source in enumerate(sources):

                @pl.when(place // per == m)
                def _(source=source, place=place - m * per, p=p, k=k):
                    strip_copy(source, place, window, sems, p, k).start()


def await_fetch(sources, window, sems, patches):
    for p in range(patches):
        for k in range(WIN):
            strip_copy(sources[0], 0, window, sems, p, k).wait()


def patch_rows(meta, window, p, k):
    top, left = meta[p, 0], meta[p, 1]
    low = row_of_lane((BSIDE, PATCH)) < top
    out = []
    for c in range(2):

        def pick(slot):
            strip = window[p, slot, c].astype(F32)
            return jnp.where(low, strip[:, PATCH:], strip[:, :PATCH])

        value = pick(k)
        if k == 0:
            b = lax.broadcasted_iota(jnp.int32, (BSIDE, PATCH), 0)
            value = jnp.where(b < left, pick(WIN - 1), value)
        out.append(value)
    return out


def propagate(field, half, right, left, patches, put):
    for p in range(patches):
        y = dot(field[cols(p), :], right[...])
        for c in range(2):
            half[cols(c), cols(p)] = y[:, c * PATCH : (c + 1) * PATCH].astype(BF16)
    for c in range(2):
        put(c, dot(left[cols(c), :], half[...]))


def add_gradient(meta, grid, p, k, pair):
    top, left = meta[p, 0], meta[p, 1]
    low = row_of_lane((BSIDE, PATCH)) < top
    b = lax.broadcasted_iota(jnp.int32, (BSIDE, PATCH), 0)

    def put(slot, c, value):
        place = meta[p, 2 + WIN + slot]
        for half in range(2):
            piece = jnp.where(low if half else jnp.logical_not(low), value, 0.0)
            spot = (place, c, slice(None), slice(half * PATCH, (half + 1) * PATCH))
            if p > 0 or slot == WIN - 1:
                piece = piece + grid[spot].astype(F32)
            grid[spot] = piece.astype(BF16)

    if k > 0:
        for c in range(2):
            put(k, c, pair[c])
        return
    for c in range(2):
        put(0, c, jnp.where(b < left, 0.0, pair[c]))

    @pl.when(left > 0)
    def _():
        for c in range(2):
            put(WIN - 1, c, jnp.where(b < left, pair[c], 0.0))


def send_out(grid, outs, sems):
    start = 0
    copies = []
    for n, out in enumerate(outs):
        size = out.shape[0]
        copies.append(pltpu.make_async_copy(grid.at[pl.ds(start, size)], out, sems.at[n]))
        start += size
    for copy in copies:
        copy.start()
    return copies


def rows(k):
    return pl.ds(k * BSIDE, BSIDE)


def at_rows(c, k):
    return pl.ds(c * PATCH + k * BSIDE, BSIDE)


def any_spec():
    return pl.BlockSpec(memory_space=pl.ANY)


def vmem_spec():
    return pl.BlockSpec(memory_space=pltpu.VMEM)


def smem_spec():
    return pl.BlockSpec(memory_space=pltpu.SMEM)


def params():
    return pltpu.CompilerParams(vmem_limit_bytes=VMEM_BYTES)


def cost(microseconds):
    return pl.CostEstimate(flops=0, bytes_accessed=int(microseconds * SCALE), transcendentals=0)


def wrap_exact(value, mx, my):
    high = value.astype(BF16)
    rest = value - high.astype(F32)
    middle = rest.astype(BF16)
    low = (rest - middle.astype(F32)).astype(BF16)
    high, middle, low = (dot(dot_nt(mx, part).astype(BF16), my) for part in (high, middle, low))
    return high + (middle + low)


def forward(layer, meta, sources, before, right, left, patches):
    wide = patches * PATCH

    n = len(sources)

    def kernel(meta, *refs):
        sources, (before, right, left, trans, after), refs = refs[:n], refs[n : n + 5], refs[n + 5 :]
        fetch(meta, sources, window := refs[-4], sems := refs[-1], patches)
        field, half = refs[-3:-1]
        if layer == 0:
            probe, before = before, refs[0]
            for p in range(patches):
                my, mx = shifts(meta, p)
                for c in range(2):
                    before[p, c] = wrap_exact(probe[c], mx, my)
        await_fetch(sources, window, sems, patches)
        for p in range(patches):
            for k in range(PATCH // BSIDE):
                tr, ti = patch_rows(meta, window, p, k)
                trans[at_rows(0, k), cols(p)] = tr.astype(BF16)
                trans[at_rows(1, k), cols(p)] = ti.astype(BF16)
                tr = tr + 1.0
                if layer == 0:
                    fr, fi = before[p, 0, rows(k), :], before[p, 1, rows(k), :]
                else:
                    fr = before[at_rows(0, k), cols(p)].astype(F32)
                    fi = before[at_rows(1, k), cols(p)].astype(F32)
                field[at_rows(p, k), cols(0)] = (tr * fr - ti * fi).astype(BF16)
                field[at_rows(p, k), cols(1)] = (tr * fi + ti * fr).astype(BF16)

        def put(c, value):
            after[cols(c), :] = value.astype(BF16)

        propagate(field, half, right, left, patches, put)

    plane = jax.ShapeDtypeStruct((2 * PATCH, wide), BF16)
    extra = [jax.ShapeDtypeStruct((patches, 2, PATCH, PATCH), F32)] if layer == 0 else []
    return pl.pallas_call(
        kernel,
        out_shape=[plane, plane, *extra],
        in_specs=[smem_spec()] + [any_spec()] * n + [vmem_spec()] * 3,
        out_specs=[vmem_spec()] * (2 + len(extra)),
        scratch_shapes=[
            pltpu.VMEM((patches, WIN, 2, BSIDE, TALL), BF16),
            pltpu.VMEM((wide, 2 * PATCH), BF16),
            pltpu.VMEM((2 * PATCH, wide), BF16),
            pltpu.SemaphoreType.DMA((patches, WIN)),
        ],
        compiler_params=params(),
        cost_estimate=cost(3.5),
        name=f"forward_{layer}",
    )(meta, *sources, before, right, left)


def back_step(meta, p, k, g, q, t, grid, field):
    gr, gi = g
    qr, qi = q
    tr, ti = t
    add_gradient(meta, grid, p, k, (gr * qr + gi * qi, gi * qr - gr * qi))
    field[at_rows(p, k), cols(0)] = (tr * gr + ti * gi).astype(BF16)
    field[at_rows(p, k), cols(1)] = (ti * gr - tr * gi).astype(BF16)


def clear(grid):
    @pl.loop(0, grid.shape[0])
    def _(n):
        grid[n] = jnp.zeros(grid.shape[1:], BF16)


def put_conjugate(out):
    def put(c, value):
        out[cols(c), :] = (-value if c else value).astype(BF16)

    return put


def through_slice(meta, window, load, trans, field, patches):
    for p in range(patches):
        for k in range(PATCH // BSIDE):
            tr, ti = patch_rows(meta, window, p, k)
            trans[at_rows(0, k), cols(p)] = tr.astype(BF16)
            trans[at_rows(1, k), cols(p)] = ti.astype(BF16)
            tr = tr + 1.0
            fr, fi = load(p, 0, k), load(p, 1, k)
            field[at_rows(p, k), cols(0)] = (tr * fr - ti * fi).astype(BF16)
            field[at_rows(p, k), cols(1)] = (tr * fi + ti * fr).astype(BF16)


def loader(ref):
    return lambda p, c, k: ref[at_rows(c, k), cols(p)].astype(F32)


def put_plain(out):
    def put(c, value):
        out[cols(c), :] = value.astype(BF16)

    return put


def dft_pair(half, other, left, right, patches, use):
    for c in range(2):
        y = dot(left[cols(c), :], half[...])
        for p in range(patches):
            other[cols(p), cols(c)] = y[:, p * PATCH : (p + 1) * PATCH].astype(BF16)
    for p in range(patches):
        use(p, dot(other[cols(p), :], right[...]))


def turn(metas, groups, carried, amplitudes, tabs, pieces, patches):
    wide = patches * PATCH
    n_out = len(pieces)
    n2, n3 = len(groups[0]), len(groups[1])

    def kernel(meta, meta_last, *refs):
        given2, given3, refs = refs[:n2], refs[n2 : n2 + n3], refs[n2 + n3 :]
        q2, measured, hr, hl, fl, fr = refs[:6]
        outs, refs = refs[6 : 6 + 2 * n_out], refs[6 + 2 * n_out :]
        after, windows, t2, t3, q3, adjoint, field, half, other, grids, sems, out_sems = refs
        fetch(meta, given2, windows.at[0], sems.at[0], patches)
        fetch(meta_last, given3, windows.at[1], sems.at[1], patches)
        clear(grids.at[0])
        clear(grids.at[1])
        await_fetch(given2, windows.at[0], sems.at[0], patches)
        through_slice(meta, windows.at[0], loader(q2), t2, field, patches)
        propagate(field, half, hr, hl, patches, put_plain(q3))
        await_fetch(given3, windows.at[1], sems.at[1], patches)
        through_slice(meta_last, windows.at[1], loader(q3), t3, field, patches)
        moves = [shifts(meta, p) for p in range(patches)]
        for p, (my, mx) in enumerate(moves):
            for c in range(2):
                turned = dot_nt(my, field[cols(p), cols(c)]).astype(BF16)
                half[cols(c), cols(p)] = dot(turned, mx).astype(BF16)

        def misfit(p, far):
            real, imag = far[:, :PATCH], far[:, PATCH:]
            modulus = jnp.sqrt(real * real + imag * imag)
            keeping = 1.0 - measured[p] / jnp.maximum(modulus, FLOOR)
            half[cols(0), cols(p)] = (real * keeping).astype(BF16)
            half[cols(1), cols(p)] = (-imag * keeping).astype(BF16)

        def wrapped(p, g):
            my, mx = moves[p]
            for c in range(2):
                part = g[:, c * PATCH : (c + 1) * PATCH]
                part = (-part if c else part).astype(BF16)
                adjoint[cols(c), cols(p)] = dot(dot_nt(mx, part).astype(BF16), my).astype(BF16)

        dft_pair(half, other, fl, fr, patches, misfit)
        dft_pair(half, other, fl, fr, patches, wrapped)

        def copies(layer):
            found, start = [], 0
            for n, size in enumerate(pieces):
                found.append(
                    pltpu.make_async_copy(
                        grids.at[layer, pl.ds(start, size)],
                        outs[layer * n_out + n],
                        out_sems.at[layer, n],
                    )
                )
                start += size
            return found

        g = loader(adjoint)
        for layer, spot, q, t, nxt in (
            (1, meta_last, loader(q3), loader(t3), adjoint),
            (0, meta, loader(q2), loader(t2), after),
        ):
            for p in range(patches):
                for k in range(PATCH // BSIDE):
                    back_step(
                        spot,
                        p,
                        k,
                        (g(p, 0, k), g(p, 1, k)),
                        (q(p, 0, k), q(p, 1, k)),
                        (t(p, 0, k) + 1.0, t(p, 1, k)),
                        grids.at[layer],
                        field,
                    )
            for copy in copies(layer):
                copy.start()
            propagate(field, half, hr, hl, patches, put_conjugate(nxt))
        for layer in range(2):
            for copy in copies(layer):
                copy.wait()

    plane = pltpu.VMEM((2 * PATCH, wide), BF16)
    strips = [jax.ShapeDtypeStruct((n, 2, BSIDE, TALL), BF16) for n in pieces]
    *outs, after = pl.pallas_call(
        kernel,
        out_shape=(*strips * 2, jax.ShapeDtypeStruct((2 * PATCH, wide), BF16)),
        in_specs=[smem_spec()] * 2 + [any_spec()] * (n2 + n3) + [vmem_spec()] * 6,
        out_specs=(*[any_spec()] * (2 * n_out), vmem_spec()),
        scratch_shapes=[
            pltpu.VMEM((2, patches, WIN, 2, BSIDE, TALL), BF16),
            plane,
            plane,
            plane,
            plane,
            pltpu.VMEM((wide, 2 * PATCH), BF16),
            plane,
            pltpu.VMEM((wide, 2 * PATCH), BF16),
            pltpu.VMEM((2, sum(pieces), 2, BSIDE, TALL), BF16),
            pltpu.SemaphoreType.DMA((2, patches, WIN)),
            pltpu.SemaphoreType.DMA((2, n_out)),
        ],
        compiler_params=params(),
        cost_estimate=cost(11.5),
        name="turn",
    )(*metas, *groups[0], *groups[1], carried, amplitudes, *tabs)
    return outs[:n_out], outs[n_out:], after


def backward(layer, meta, adjoint, carried, trans, right, left, pieces, patches):
    wide = patches * PATCH
    n_out = len(pieces)

    def kernel(meta, adjoint, carried, trans, right, left, *refs):
        outs, refs = refs[:n_out], refs[n_out:]
        after, field, half, grid, out_sems = refs
        clear(grid)
        for p in range(patches):
            for k in range(PATCH // BSIDE):
                load = lambda ref, c: ref[at_rows(c, k), cols(p)].astype(F32)
                back_step(
                    meta,
                    p,
                    k,
                    (load(adjoint, 0), load(adjoint, 1)),
                    (load(carried, 0), load(carried, 1)),
                    (load(trans, 0) + 1.0, load(trans, 1)),
                    grid,
                    field,
                )
        copies = send_out(grid, outs, out_sems)
        propagate(field, half, right, left, patches, put_conjugate(after))
        for copy in copies:
            copy.wait()

    plane = jax.ShapeDtypeStruct((2 * PATCH, wide), BF16)
    strips = [jax.ShapeDtypeStruct((n, 2, BSIDE, TALL), BF16) for n in pieces]
    *outs, after = pl.pallas_call(
        kernel,
        out_shape=(*strips, plane),
        in_specs=[smem_spec()] + [vmem_spec()] * 5,
        out_specs=(*[any_spec()] * n_out, vmem_spec()),
        scratch_shapes=[
            pltpu.VMEM((wide, 2 * PATCH), BF16),
            pltpu.VMEM((2 * PATCH, wide), BF16),
            pltpu.VMEM((sum(pieces), 2, BSIDE, TALL), BF16),
            pltpu.SemaphoreType.DMA((n_out,)),
        ],
        compiler_params=params(),
        cost_estimate=cost(2.3),
        name=f"backward_{layer}",
    )(meta, adjoint, carried, trans, right, left)
    return outs, after


def first_slice(meta, adjoint, probe, trans, pieces, patches):
    wide = patches * PATCH
    n_out = len(pieces)

    def kernel(meta, adjoint, probe, trans, *refs):
        outs, refs = refs[:n_out], refs[n_out:]
        total, field, grid, out_sems = refs
        clear(grid)
        for p in range(patches):
            for k in range(PATCH // BSIDE):
                load = lambda ref, c: ref[at_rows(c, k), cols(p)].astype(F32)
                gr, gi = load(adjoint, 0), load(adjoint, 1)
                tr, ti = load(trans, 0) + 1.0, load(trans, 1)
                pr, pi = probe[p, 0, rows(k), :], probe[p, 1, rows(k), :]
                add_gradient(meta, grid, p, k, (gr * pr + gi * pi, gi * pr - gr * pi))
                field[at_rows(p, k), cols(0)] = (gr * tr + gi * ti).astype(BF16)
                field[at_rows(p, k), cols(1)] = (gi * tr - gr * ti).astype(BF16)
        copies = send_out(grid, outs, out_sems)
        moves = [shifts(meta, p) for p in range(patches)]
        for c in range(2):
            terms = [
                dot(dot_nt(my, field[cols(p), cols(c)]).astype(BF16), mx)
                for p, (my, mx) in enumerate(moves)
            ]
            total[c] = sum(terms[1:], terms[0]).astype(BF16)
        for copy in copies:
            copy.wait()

    strips = [jax.ShapeDtypeStruct((n, 2, BSIDE, TALL), BF16) for n in pieces]
    *outs, total = pl.pallas_call(
        kernel,
        out_shape=(*strips, jax.ShapeDtypeStruct((2, PATCH, PATCH), BF16)),
        in_specs=[smem_spec()] + [vmem_spec()] * 3,
        out_specs=(*[any_spec()] * n_out, vmem_spec()),
        scratch_shapes=[
            pltpu.VMEM((wide, 2 * PATCH), BF16),
            pltpu.VMEM((sum(pieces), 2, BSIDE, TALL), BF16),
            pltpu.SemaphoreType.DMA((n_out,)),
        ],
        compiler_params=params(),
        cost_estimate=cost(2.3),
        name="first_slice",
    )(meta, adjoint, probe, trans)
    return outs, total


def lane_group(shape):
    return lax.broadcasted_iota(jnp.int32, shape, 1) // BSIDE


def to_strips(blocks):
    flat = blocks.reshape(-1, BSIDE * BSIDE)

    def kernel(flat, *refs):
        outs, lanes = refs[:-1], refs[-1]
        group = lane_group((8, 128))
        for ag in range(8):
            lanes[ag] = flat[:, ag * 128 : (ag + 1) * 128]
        for s in range(SLICES):
            for t in range(2):
                tall = []
                for ag in range(8):
                    chunk = [
                        lanes[ag, pl.ds(t * 128 + band * 8 + 2 * s + c, 8, stride=16), :]
                        for band in range(2)
                        for c in range(2)
                    ]
                    for a4 in range(4):
                        value = None
                        for n in range(4):
                            move = (n - a4) % 4 * BSIDE
                            moved = pltpu.roll(chunk[n], move, 1) if move else chunk[n]
                            value = moved if n == 0 else jnp.where(group == n, moved, value)
                        tall.append(value)
                for half in range(2):
                    square = jnp.concatenate(tall[half * 16 : half * 16 + 16], axis=0)
                    square = jnp.transpose(square).astype(BF16)
                    for n in range(4):
                        outs[s][n // 2, n % 2, :, pl.ds(t * PATCH + half * 128, 128)] = square[
                            n * BSIDE : (n + 1) * BSIDE
                        ]

    return pl.pallas_call(
        kernel,
        out_shape=[jax.ShapeDtypeStruct((2, 2, BSIDE, TALL), BF16)] * SLICES,
        in_specs=[vmem_spec()],
        out_specs=[vmem_spec()] * SLICES,
        scratch_shapes=[pltpu.VMEM((8, flat.shape[0], 128), F32)],
        compiler_params=params(),
        cost_estimate=cost(1.5),
        name="to_strips",
    )(flat)


def to_blocks(terms):
    counts = [len(term) for term in terms]

    def kernel(*refs):
        out, lanes = refs[-2:]
        group = lane_group((8, 128))
        start = 0
        for s in range(SLICES):
            parts = refs[start : start + counts[s]]
            start += counts[s]
            for t in range(2):
                for half in range(2):
                    pieces = []
                    for n in range(4):
                        spot = (n // 2, n % 2, slice(None), pl.ds(t * PATCH + half * 128, 128))
                        value = parts[0][spot].astype(F32)
                        for part in parts[1:]:
                            value = value + part[spot].astype(F32)
                        pieces.append(value)
                    tall = jnp.transpose(jnp.concatenate(pieces, axis=0))
                    for g in range(4):
                        chunk = [tall[(g * 4 + a4) * 8 : (g * 4 + a4) * 8 + 8] for a4 in range(4)]
                        ag = half * 4 + g
                        for n in range(4):
                            value = None
                            for a4 in range(4):
                                move = (a4 - n) % 4 * BSIDE
                                moved = pltpu.roll(chunk[a4], move, 1) if move else chunk[a4]
                                value = moved if a4 == 0 else jnp.where(group == a4, moved, value)
                            row = t * 128 + n // 2 * 8 + 2 * s + n % 2
                            lanes[ag, pl.ds(row, 8, stride=16), :] = value
        for ag in range(8):
            out[:, ag * 128 : (ag + 1) * 128] = lanes[ag]

    flat = [part for term in terms for part in term]
    out = pl.pallas_call(
        kernel,
        out_shape=jax.ShapeDtypeStruct((FOOT * COL_BANDS * 2 * SLICES, BSIDE * BSIDE), F32),
        in_specs=[vmem_spec()] * len(flat),
        out_specs=vmem_spec(),
        scratch_shapes=[pltpu.VMEM((8, FOOT * COL_BANDS * 2 * SLICES, 128), F32)],
        compiler_params=params(),
        cost_estimate=cost(1.5),
        name="to_blocks",
    )(*flat)
    return out.reshape(FOOT * COL_BANDS, 2 * SLICES, BSIDE * BSIDE)


def after(value, *events):
    return lax.optimization_barrier((value, *events))[0]


def describe(top, left, source_of, target_of, last):
    first = left // BSIDE
    strips = jnp.minimum(first[:, None] + jnp.arange(WIN, dtype=jnp.int32)[None, :], last)
    columns = [top[:, None], (left % BSIDE)[:, None], source_of(strips), target_of(strips)]
    return jnp.concatenate(columns, axis=1).astype(jnp.int32)


FAR, NEAR, OVER_Y, OVER_CORE = 8, 4, 2, 1


def swap(value, bit):
    return lax.ppermute(value, "scan", [(i, i ^ bit) for i in range(16)])


def stage(moves, *events):
    values = lax.optimization_barrier((*(value for value, _ in moves), *events))
    return [swap(value, bit) for value, (_, bit) in zip(values, moves)]


def join(*values):
    return jnp.concatenate(values, axis=0)


def widen(value):
    return value.astype(F32)


def plus(value, *others):
    return sum((widen(other) for other in others), widen(value)).astype(BF16)


def slots(owner, order):
    bits = [(owner & bit) // bit * 2**n for n, bit in enumerate(order)]
    return sum(bits[1:], bits[0])


LINE_FIRST = (FAR, NEAR, OVER_Y, OVER_CORE)
PLANE_FIRST = (OVER_Y, FAR, NEAR, OVER_CORE)


def sum_probe(total, n_terms, events):
    me = lax.axis_index("scan")
    core, y = me % 2, me // 2 % 2
    mine = jnp.where(core == 0, total[0], total[1])
    theirs = jnp.where(core == 0, total[1], total[0])
    mine = plus(mine, swap(after(theirs, *events[0]), OVER_CORE))
    mine = mine.reshape(2, PATCH // 2, PATCH)
    theirs = jnp.where(y == 0, mine[1], mine[0])
    mine = jnp.where(y == 0, mine[0], mine[1])
    mine = plus(mine, swap(after(theirs, *events[1]), OVER_Y))
    mine = plus(mine, swap(after(mine, *events[2]), NEAR))
    mine = (widen(mine) + widen(swap(after(mine, *events[3]), FAR))) / math.sqrt(n_terms)
    other = swap(after(mine, *events[4]), OVER_Y)
    mine = jnp.where(y == 0, join(mine, other), join(other, mine))
    other = swap(after(mine, *events[5]), OVER_CORE)
    return jnp.where(core == 0, jnp.stack([mine, other]), jnp.stack([other, mine]))


OPT = {"k0":0,"B":1,"kb1":2,"y2s":1,"first":1,"line3":1,"far0":1,"probe":("none","none","near2","far2","near0","none")}


def pick(name, default=0):
    return OPT.get(name, default)


def on_small(object_blocks, probe, positions, anchors, amplitudes):
    me = lax.axis_index("scan")
    corner = anchors[0] * BSIDE
    patches = positions.shape[0]

    def described(order):
        def place(strips):
            return slots(strips % OWN_COLS ^ me, order) * COL_BANDS + strips // OWN_COLS

        return describe(
            positions[:, 0] + corner[0],
            positions[:, 1] + corner[1],
            place,
            place,
            OWN_COLS * COL_BANDS - 1,
        )

    meta, meta_last = described(LINE_FIRST), described(PLANE_FIRST)
    hr, hl, fl, fr = tables()
    own = to_strips(object_blocks)

    far0, ys = stage([(own[0], FAR), (join(*own), OVER_Y)])
    far13 = join(own[1], own[3]) if pick("B") == 1 else own[1]
    far1, near0 = stage([(far13, FAR), (join(own[0], far0), NEAR)])
    far1, far3 = far1[:2], far1[2:]
    far2, near1, y0 = stage(
        [(own[2], FAR), (join(own[1], far1), NEAR), (join(far0, near0), OVER_Y)], ys, *([meta, meta_last] if pick("meta", 1) else [])
    )
    pair3 = join(own[3], ys[6:])
    here0 = join(own[0], far0, near0, ys[:2], y0)
    core0, near2, y1, far3y = stage(
        [
            (here0, OVER_CORE),
            (join(own[2], far2), NEAR),
            (join(far1, near1), OVER_Y),
            (ys[6:] if pick("B") == 1 else pair3, FAR),
        ],
    )
    if pick("B") == 1:
        far3 = join(far3, far3y)
    else:
        far3 = far3y
    here1 = join(own[1], far1, near1, ys[2:4], y1)
    here3 = join(pair3, far3)
    if pick("k0", 1):
        trans0, q1, probes = forward(0, meta, (here0, core0), probe, hr, hl, patches)
        core1, y2, near3 = stage(
            [(here1, OVER_CORE), (join(far2, near2), OVER_Y), (here3, NEAR)], q1
        )
    else:
        core1, y2, near3 = stage(
            [(here1, OVER_CORE), (join(far2, near2), OVER_Y), (here3, NEAR)], core0
        )
        trans0, q1, probes = forward(0, meta, (here0, core0), probe, hr, hl, patches)
    trans1, q2 = forward(1, meta, (here1, core1), q1, hr, hl, patches)
    here2 = join(own[2], far2, near2, ys[4:6], y2)
    core3a = swap(after(here3, *[(q1,), (), (q2,), (core1,)][pick("core3a")]), OVER_CORE)
    if pick("core2") == 0:
        core3b, core2 = stage([(near3, OVER_CORE), (here2, OVER_CORE)], q2)
    elif pick("core2") == 1:
        core2 = swap(after(here2, near3), OVER_CORE)
        core3b = swap(after(near3, y2), OVER_CORE)
    else:
        core2 = swap(after(here2, q2), OVER_CORE)
        core3b = swap(near3, OVER_CORE)
    pieces = (8, 8, 16)
    (here2, over2, core2), (here3, near3, core3), g1 = turn(
        (meta, meta_last),
        ((here2, core2), (here3, near3, core3a, core3b)),
        q2,
        amplitudes,
        (hr, hl, fl, fr),
        pieces,
        patches,
    )

    came3 = swap(core3, OVER_CORE)
    came2 = swap(core2, OVER_CORE)
    near3 = plus(near3, came3[8:])
    if pick("near3s"):
        near3 = swap(after(near3, g1), NEAR)
    events = [(came3,), (came2, near3), (), (near3,)][0 if pick("near3s") else pick("kb1")]
    (here1, over1, core1), g0 = backward(
        1, meta, after(g1, *events), q1, trans1, hr, hl, pieces, patches
    )
    came1 = swap(core1, OVER_CORE)
    y2 = after(plus(over2[2:], came2[10:]), *[(g0,), ()][pick("y2s")])
    y1 = plus(over1[2:], came1[10:])
    base3 = plus(here3, came3[:8])
    events = [(y2, came1), (y2, y1, base3), (came1,), (y2, came1, base3), (y2,)][pick("first")]
    (here0, over0, core0), total = first_slice(
        meta, after(g0, *events), probes, trans0, pieces, patches
    )
    if not pick("near3s"):
        near3 = swap(near3, NEAR)
    y2 = swap(y2, OVER_Y)
    came0 = swap(core0, OVER_CORE)
    y0 = plus(over0[2:], came0[10:])
    if pick("line3") == 0:
        line3 = plus(here3, came3[:8], near3)
        head3, tail3 = (line3[:4],), line3[4:]
    else:
        head3, tail3 = (base3[:4], near3[:4]), plus(base3[4:], near3[4:])
    line2 = plus(here2[2:], came2[2:8], y2)
    near2, y1, far3 = stage(
        [(line2[2:], NEAR), (y1, OVER_Y), (tail3[2:] if pick("C") else tail3, FAR)], *[(y0,), ()][pick("s4")]
    )
    line1 = plus(here1[2:], came1[2:8], y1)
    out2 = plus(line2[:2], near2[2:])
    if pick("C"):
        out2 = join(out2, tail3[:2])
    far2, near1, y0 = stage(
        [(out2, FAR), (line1[2:], NEAR), (y0, OVER_Y)]
    )
    if pick("C"):
        far2, far3 = far2[:2], join(far2[2:], far3)
    pair3 = plus(*head3, far3)
    line0 = plus(here0[2:], came0[2:8], y0)
    rest = [
        plus(over0[:2], came0[8:10]),
        plus(over1[:2], came1[8:10]),
        plus(over2[:2], came2[8:10]),
    ]
    far1, near0, ys = stage(
        [
            (plus(line1[:2], near1[2:]), FAR),
            (line0[2:], NEAR),
            (join(*rest, pair3[2:]), OVER_Y),
        ],
        far2,
    )
    far0 = swap(after(plus(line0[:2], near0[2:]), *[(), (far1,)][pick("far0")]), FAR)
    marks = {
        "none": (),
        "came0": (came0,),
        "y2": (y2,),
        "near3": (near3,),
        "y1": (y1,),
        "near2": (near2,),
        "far3": (far3,),
        "far2": (far2,),
        "near1": (near1,),
        "y0": (y0,),
        "near0": (near0,),
        "far1": (far1,),
        "ys": (ys,),
    }
    when = [marks[name] for name in pick("probe", ("came0", "y2", "y1", "y0", "near0", "near0"))]
    probe_gradient = sum_probe(
        total, lax.axis_size("scan") * patches, when
    )
    if pick("tail"):
        far0 = after(far0, probe_gradient)
    terms = [
        (here0[:2], came0[:2], near0[:2], ys[:2], far0),
        (here1[:2], came1[:2], near1[:2], ys[2:4], far1),
        (here2[:2], came2[:2], near2[:2], ys[4:6], far2),
        (pair3[:2], ys[6:]),
    ]
    return (to_blocks(terms), probe_gradient)


def footprint_slots(anchor_row, anchor_col, target, slot_number, own_rows):
    per_col = FOOT // OWN_COLS
    first_row = (target // OWN_COLS - anchor_row) % own_rows
    first_col = (target % OWN_COLS - anchor_col) % OWN_COLS
    inner_row = first_row + own_rows * (slot_number // per_col)
    inner_col = first_col + OWN_COLS * (slot_number % per_col)
    row_block = anchor_row + inner_row
    col_block = anchor_col + inner_col
    local = row_block // own_rows * COL_BANDS + col_block // OWN_COLS
    return (inner_row * FOOT + inner_col, local)


def work(meta, sources, probe, amplitudes, pieces):
    patches = amplitudes.shape[0]
    hr, hl, fl, fr = tables()
    t0, q1, probes = forward(0, meta, sources[0], probe, hr, hl, patches)
    t1, q2 = forward(1, meta, sources[1], q1, hr, hl, patches)
    grad2, grad3, g1 = turn(
        (meta, meta), sources[2:], q2, amplitudes, (hr, hl, fl, fr), pieces, patches
    )
    grad1, g0 = backward(1, meta, g1, q1, t1, hr, hl, pieces, patches)
    grad0, total = first_slice(meta, g0, probes, t0, pieces, patches)
    return [grad0, grad1, grad2, grad3], total


def on_any(object_blocks, probe, positions, anchors, amplitudes):
    n_scan = lax.axis_size("scan")
    own_rows = n_scan // OWN_COLS
    capacity = FOOT * FOOT // n_scan
    per_col = FOOT // OWN_COLS
    channels = object_blocks.shape[1]
    anchor_row = anchors[0, 0]
    anchor_col = anchors[0, 1]
    targets = jnp.arange(n_scan, dtype=jnp.int32)[:, None]
    slots = jnp.arange(capacity, dtype=jnp.int32)[None, :]
    send_order, wanted = footprint_slots(anchor_row, anchor_col, targets, slots, own_rows)
    inner = jnp.arange(FOOT, dtype=jnp.int32)
    inner_row = inner[:, None]
    inner_col = inner[None, :]
    holder = (anchor_row + inner_row) % own_rows * OWN_COLS + (anchor_col + inner_col) % OWN_COLS
    arrival = (holder * capacity + inner_row // own_rows * per_col + inner_col // OWN_COLS).reshape(
        -1
    )
    stored = object_blocks.astype(BF16)
    asked = lax.all_to_all(wanted, "scan", split_axis=0, concat_axis=0, tiled=True)
    found = jnp.take(stored, asked, axis=0)
    received = lax.all_to_all(found, "scan", split_axis=0, concat_axis=0, tiled=True)
    footprint = jnp.take(
        received.reshape(n_scan * capacity, channels, BSIDE * BSIDE), arrival, axis=0
    )
    strips = (
        footprint.reshape(2, 8, FOOT, SLICES, 2, BSIDE, BSIDE)
        .transpose(3, 2, 4, 6, 0, 5, 1)
        .reshape(SLICES, FOOT, 2, BSIDE, TALL)
    )
    meta = describe(
        positions[:, 0], positions[:, 1], lambda strips: strips, lambda strips: strips, FOOT - 1
    )
    sources = [(strips[s],) for s in range(SLICES)]
    grads, total = work(meta, sources, probe, amplitudes, (FOOT,))
    blocked = (
        jnp.stack([grad[0] for grad in grads])
        .reshape(SLICES, FOOT, 2, BSIDE, 2, BSIDE, 8)
        .transpose(4, 6, 1, 0, 2, 5, 3)
        .reshape(FOOT * FOOT, channels, BSIDE * BSIDE)
    )
    outgoing = jnp.take(blocked, send_order.reshape(-1), axis=0).reshape(
        n_scan, capacity, channels, BSIDE * BSIDE
    )
    incoming = lax.all_to_all(outgoing, "scan", split_axis=0, concat_axis=0, tiled=True)
    owned = jnp.arange(object_blocks.shape[0], dtype=jnp.int32)
    selector = (asked.reshape(-1)[:, None] == owned[None, :]).astype(F32)
    object_gradient = jnp.einsum(
        "sk,scb->kcb",
        selector,
        incoming.reshape(n_scan * capacity, channels, BSIDE * BSIDE).astype(F32),
        precision=lax.Precision.HIGHEST,
    )
    summed = lax.psum(widen(total), "scan")
    return (object_gradient, summed / math.sqrt(n_scan * positions.shape[0]))


def solution(mesh):
    in_specs = (
        P(("group", "scan"), None, None),
        P("group", None, None),
        P(("group", "scan"), None),
        P(("group", "scan"), None),
        P(("group", "scan"), None, None),
    )
    out_specs = (P(("group", "scan"), None, None), P("group", None, None))
    small = mesh.shape["scan"] == OWN_COLS
    return jax.shard_map(
        on_small if small else on_any,
        mesh=mesh,
        in_specs=in_specs,
        out_specs=out_specs,
        check_vma=False,
    )
```

```python
import math

import jax
import jax.numpy as jnp
import numpy as np
from jax import lax
from jax.experimental import pallas as pl
from jax.experimental.pallas import tpu as pltpu
from jax.sharding import PartitionSpec as P

PATCH = 256
SLICES = 4
BSIDE = 32
FOOT = 16
OWN_COLS = 16
COL_BANDS = 2
FLOOR = 0.25
WIN = 9
TALL = FOOT * BSIDE
VMEM_BYTES = 16 * 1024 * 1024
SCALE = 3.6e6
F32 = jnp.float32
BF16 = jnp.bfloat16


def lane_rows():
    lane = np.arange(PATCH)
    return lane % 8 * BSIDE + lane // 8


def stacked_right(table):
    real, imag = table
    return np.block([[real, imag], [-imag, real]])


def stacked_left(table):
    real, imag = table
    return np.block([[real, -imag], [imag, real]])


def tables():
    counter = np.arange(PATCH)
    turns = counter[:, None] * counter[None, :] % PATCH
    angles = turns.astype(np.float64) * (2.0 * math.pi / PATCH)
    scaled = 1.0 / math.sqrt(PATCH)
    dft = (np.cos(angles) * scaled, -np.sin(angles) * scaled)
    centred = (counter + PATCH // 2) % PATCH - PATCH // 2
    turns = (4 * counter[:, None] * counter[None, :] - centred[None, :] ** 2) % (4 * PATCH)
    angles = turns.astype(np.float64) * (2.0 * math.pi / (4 * PATCH))
    gap = (counter[:, None] - counter[None, :]) % PATCH
    fresnel = ((np.cos(angles).sum(1) / PATCH)[gap], (np.sin(angles).sum(1) / PATCH)[gap])
    order = lane_rows()
    across = tuple(part.T[np.ix_(order, order)] for part in fresnel)
    down = tuple(part.T for part in fresnel)
    wanted = (
        stacked_right(across),
        stacked_left(down),
        stacked_left(dft),
        stacked_right(dft),
    )
    return tuple(jnp.asarray(t.astype(np.float32)).astype(BF16) for t in wanted)


def dot(left, right):
    return jnp.dot(left, right, preferred_element_type=F32)


def dot_nt(left, right):
    return lax.dot_general(left, right, (((1,), (1,)), ((), ())), preferred_element_type=F32)


def row_of_lane(shape):
    lane = lax.broadcasted_iota(jnp.int32, shape, 1)
    return (lane & 7) * BSIDE + (lane >> 3)


def shifts(meta, p, dtype=BF16):
    top, left = meta[p, 0], meta[p, 1]
    shape = (PATCH, PATCH)
    i = lax.broadcasted_iota(jnp.int32, shape, 0)
    j = lax.broadcasted_iota(jnp.int32, shape, 1)
    my = jnp.where(row_of_lane(shape) == ((i + top) & (PATCH - 1)), 1.0, 0.0).astype(dtype)
    mx = jnp.where(i == ((j + left) & (PATCH - 1)), 1.0, 0.0).astype(dtype)
    return my, mx


def cols(c):
    return pl.ds(c * PATCH, PATCH)


def strip_copy(source, place, window, sems, p, k):
    return pltpu.make_async_copy(source.at[place], window.at[p, k], sems.at[p, k])


def fetch(meta, sources, window, sems, patches):
    per = sources[0].shape[0]
    for p in range(patches):
        for k in range(WIN):
            place = meta[p, 2 + k]
            for m, source in enumerate(sources):

                @pl.when(place // per == m)
                def _(source=source, place=place - m * per, p=p, k=k):
                    strip_copy(source, place, window, sems, p, k).start()


def await_fetch(sources, window, sems, patches):
    for p in range(patches):
        for k in range(WIN):
            strip_copy(sources[0], 0, window, sems, p, k).wait()


def patch_rows(meta, window, p, k):
    top, left = meta[p, 0], meta[p, 1]
    low = row_of_lane((BSIDE, PATCH)) < top
    out = []
    for c in range(2):

        def pick(slot):
            strip = window[p, slot, c].astype(F32)
            return jnp.where(low, strip[:, PATCH:], strip[:, :PATCH])

        value = pick(k)
        if k == 0:
            b = lax.broadcasted_iota(jnp.int32, (BSIDE, PATCH), 0)
            value = jnp.where(b < left, pick(WIN - 1), value)
        out.append(value)
    return out


def propagate(field, half, right, left, patches, put):
    for p in range(patches):
        y = dot(field[cols(p), :], right[...])
        for c in range(2):
            half[cols(c), cols(p)] = y[:, c * PATCH : (c + 1) * PATCH].astype(BF16)
    for c in range(2):
        put(c, dot(left[cols(c), :], half[...]))


def add_gradient(meta, grid, p, k, pair):
    top, left = meta[p, 0], meta[p, 1]
    low = row_of_lane((BSIDE, PATCH)) < top
    b = lax.broadcasted_iota(jnp.int32, (BSIDE, PATCH), 0)

    def put(slot, c, value):
        place = meta[p, 2 + WIN + slot]
        for half in range(2):
            piece = jnp.where(low if half else jnp.logical_not(low), value, 0.0)
            spot = (place, c, slice(None), slice(half * PATCH, (half + 1) * PATCH))
            if p > 0 or slot == WIN - 1:
                piece = piece + grid[spot].astype(F32)
            grid[spot] = piece.astype(BF16)

    if k > 0:
        for c in range(2):
            put(k, c, pair[c])
        return
    for c in range(2):
        put(0, c, jnp.where(b < left, 0.0, pair[c]))

    @pl.when(left > 0)
    def _():
        for c in range(2):
            put(WIN - 1, c, jnp.where(b < left, pair[c], 0.0))


def send_out(grid, outs, sems):
    start = 0
    copies = []
    for n, out in enumerate(outs):
        size = out.shape[0]
        copies.append(pltpu.make_async_copy(grid.at[pl.ds(start, size)], out, sems.at[n]))
        start += size
    for copy in copies:
        copy.start()
    return copies


def rows(k):
    return pl.ds(k * BSIDE, BSIDE)


def at_rows(c, k):
    return pl.ds(c * PATCH + k * BSIDE, BSIDE)


def any_spec():
    return pl.BlockSpec(memory_space=pl.ANY)


def vmem_spec():
    return pl.BlockSpec(memory_space=pltpu.VMEM)


def smem_spec():
    return pl.BlockSpec(memory_space=pltpu.SMEM)


def params():
    return pltpu.CompilerParams(vmem_limit_bytes=VMEM_BYTES)


def cost(microseconds):
    return pl.CostEstimate(flops=0, bytes_accessed=int(microseconds * SCALE), transcendentals=0)


def wrap_exact(value, mx, my):
    high = value.astype(BF16)
    rest = value - high.astype(F32)
    middle = rest.astype(BF16)
    low = (rest - middle.astype(F32)).astype(BF16)
    high, middle, low = (dot(dot_nt(mx, part).astype(BF16), my) for part in (high, middle, low))
    return high + (middle + low)


def forward(layer, meta, sources, before, right, left, patches):
    wide = patches * PATCH

    n = len(sources)

    def kernel(meta, *refs):
        sources, (before, right, left, trans, after), refs = refs[:n], refs[n : n + 5], refs[n + 5 :]
        fetch(meta, sources, window := refs[-4], sems := refs[-1], patches)
        field, half = refs[-3:-1]
        if layer == 0:
            probe, before = before, refs[0]
            for p in range(patches):
                my, mx = shifts(meta, p)
                for c in range(2):
                    before[p, c] = wrap_exact(probe[c], mx, my)
        await_fetch(sources, window, sems, patches)
        for p in range(patches):
            for k in range(PATCH // BSIDE):
                tr, ti = patch_rows(meta, window, p, k)
                trans[at_rows(0, k), cols(p)] = tr.astype(BF16)
                trans[at_rows(1, k), cols(p)] = ti.astype(BF16)
                tr = tr + 1.0
                if layer == 0:
                    fr, fi = before[p, 0, rows(k), :], before[p, 1, rows(k), :]
                else:
                    fr = before[at_rows(0, k), cols(p)].astype(F32)
                    fi = before[at_rows(1, k), cols(p)].astype(F32)
                field[at_rows(p, k), cols(0)] = (tr * fr - ti * fi).astype(BF16)
                field[at_rows(p, k), cols(1)] = (tr * fi + ti * fr).astype(BF16)

        def put(c, value):
            after[cols(c), :] = value.astype(BF16)

        propagate(field, half, right, left, patches, put)

    plane = jax.ShapeDtypeStruct((2 * PATCH, wide), BF16)
    extra = [jax.ShapeDtypeStruct((patches, 2, PATCH, PATCH), F32)] if layer == 0 else []
    return pl.pallas_call(
        kernel,
        out_shape=[plane, plane, *extra],
        in_specs=[smem_spec()] + [any_spec()] * n + [vmem_spec()] * 3,
        out_specs=[vmem_spec()] * (2 + len(extra)),
        scratch_shapes=[
            pltpu.VMEM((patches, WIN, 2, BSIDE, TALL), BF16),
            pltpu.VMEM((wide, 2 * PATCH), BF16),
            pltpu.VMEM((2 * PATCH, wide), BF16),
            pltpu.SemaphoreType.DMA((patches, WIN)),
        ],
        compiler_params=params(),
        cost_estimate=cost(3.5),
        name=f"forward_{layer}",
    )(meta, *sources, before, right, left)


def back_step(meta, p, k, g, q, t, grid, field):
    gr, gi = g
    qr, qi = q
    tr, ti = t
    add_gradient(meta, grid, p, k, (gr * qr + gi * qi, gi * qr - gr * qi))
    field[at_rows(p, k), cols(0)] = (tr * gr + ti * gi).astype(BF16)
    field[at_rows(p, k), cols(1)] = (ti * gr - tr * gi).astype(BF16)


def clear(grid):
    @pl.loop(0, grid.shape[0])
    def _(n):
        grid[n] = jnp.zeros(grid.shape[1:], BF16)


def put_conjugate(out):
    def put(c, value):
        out[cols(c), :] = (-value if c else value).astype(BF16)

    return put


def through_slice(meta, window, load, trans, field, patches):
    for p in range(patches):
        for k in range(PATCH // BSIDE):
            tr, ti = patch_rows(meta, window, p, k)
            trans[at_rows(0, k), cols(p)] = tr.astype(BF16)
            trans[at_rows(1, k), cols(p)] = ti.astype(BF16)
            tr = tr + 1.0
            fr, fi = load(p, 0, k), load(p, 1, k)
            field[at_rows(p, k), cols(0)] = (tr * fr - ti * fi).astype(BF16)
            field[at_rows(p, k), cols(1)] = (tr * fi + ti * fr).astype(BF16)


def loader(ref):
    return lambda p, c, k: ref[at_rows(c, k), cols(p)].astype(F32)


def put_plain(out):
    def put(c, value):
        out[cols(c), :] = value.astype(BF16)

    return put


def dft_pair(half, other, left, right, patches, use):
    for c in range(2):
        y = dot(left[cols(c), :], half[...])
        for p in range(patches):
            other[cols(p), cols(c)] = y[:, p * PATCH : (p + 1) * PATCH].astype(BF16)
    for p in range(patches):
        use(p, dot(other[cols(p), :], right[...]))


def turn(metas, groups, carried, amplitudes, tabs, pieces, patches):
    wide = patches * PATCH
    n_out = len(pieces)
    n2, n3 = len(groups[0]), len(groups[1])

    def kernel(meta, meta_last, *refs):
        given2, given3, refs = refs[:n2], refs[n2 : n2 + n3], refs[n2 + n3 :]
        q2, measured, hr, hl, fl, fr = refs[:6]
        outs, refs = refs[6 : 6 + 2 * n_out], refs[6 + 2 * n_out :]
        after, windows, t2, t3, q3, adjoint, field, half, other, grids, sems, out_sems = refs
        fetch(meta, given2, windows.at[0], sems.at[0], patches)
        fetch(meta_last, given3, windows.at[1], sems.at[1], patches)
        clear(grids.at[0])
        clear(grids.at[1])
        await_fetch(given2, windows.at[0], sems.at[0], patches)
        through_slice(meta, windows.at[0], loader(q2), t2, field, patches)
        propagate(field, half, hr, hl, patches, put_plain(q3))
        await_fetch(given3, windows.at[1], sems.at[1], patches)
        through_slice(meta_last, windows.at[1], loader(q3), t3, field, patches)
        moves = [shifts(meta, p) for p in range(patches)]
        for p, (my, mx) in enumerate(moves):
            for c in range(2):
                turned = dot_nt(my, field[cols(p), cols(c)]).astype(BF16)
                half[cols(c), cols(p)] = dot(turned, mx).astype(BF16)

        def misfit(p, far):
            real, imag = far[:, :PATCH], far[:, PATCH:]
            modulus = jnp.sqrt(real * real + imag * imag)
            keeping = 1.0 - measured[p] / jnp.maximum(modulus, FLOOR)
            half[cols(0), cols(p)] = (real * keeping).astype(BF16)
            half[cols(1), cols(p)] = (-imag * keeping).astype(BF16)

        def wrapped(p, g):
            my, mx = moves[p]
            for c in range(2):
                part = g[:, c * PATCH : (c + 1) * PATCH]
                part = (-part if c else part).astype(BF16)
                adjoint[cols(c), cols(p)] = dot(dot_nt(mx, part).astype(BF16), my).astype(BF16)

        dft_pair(half, other, fl, fr, patches, misfit)
        dft_pair(half, other, fl, fr, patches, wrapped)

        def copies(layer):
            found, start = [], 0
            for n, size in enumerate(pieces):
                found.append(
                    pltpu.make_async_copy(
                        grids.at[layer, pl.ds(start, size)],
                        outs[layer * n_out + n],
                        out_sems.at[layer, n],
                    )
                )
                start += size
            return found

        g = loader(adjoint)
        for layer, spot, q, t, nxt in (
            (1, meta_last, loader(q3), loader(t3), adjoint),
            (0, meta, loader(q2), loader(t2), after),
        ):
            for p in range(patches):
                for k in range(PATCH // BSIDE):
                    back_step(
                        spot,
                        p,
                        k,
                        (g(p, 0, k), g(p, 1, k)),
                        (q(p, 0, k), q(p, 1, k)),
                        (t(p, 0, k) + 1.0, t(p, 1, k)),
                        grids.at[layer],
                        field,
                    )
            for copy in copies(layer):
                copy.start()
            propagate(field, half, hr, hl, patches, put_conjugate(nxt))
        for layer in range(2):
            for copy in copies(layer):
                copy.wait()

    plane = pltpu.VMEM((2 * PATCH, wide), BF16)
    strips = [jax.ShapeDtypeStruct((n, 2, BSIDE, TALL), BF16) for n in pieces]
    *outs, after = pl.pallas_call(
        kernel,
        out_shape=(*strips * 2, jax.ShapeDtypeStruct((2 * PATCH, wide), BF16)),
        in_specs=[smem_spec()] * 2 + [any_spec()] * (n2 + n3) + [vmem_spec()] * 6,
        out_specs=(*[any_spec()] * (2 * n_out), vmem_spec()),
        scratch_shapes=[
            pltpu.VMEM((2, patches, WIN, 2, BSIDE, TALL), BF16),
            plane,
            plane,
            plane,
            plane,
            pltpu.VMEM((wide, 2 * PATCH), BF16),
            plane,
            pltpu.VMEM((wide, 2 * PATCH), BF16),
            pltpu.VMEM((2, sum(pieces), 2, BSIDE, TALL), BF16),
            pltpu.SemaphoreType.DMA((2, patches, WIN)),
            pltpu.SemaphoreType.DMA((2, n_out)),
        ],
        compiler_params=params(),
        cost_estimate=cost(11.5),
        name="turn",
    )(*metas, *groups[0], *groups[1], carried, amplitudes, *tabs)
    return outs[:n_out], outs[n_out:], after


def backward(layer, meta, adjoint, carried, trans, right, left, pieces, patches):
    wide = patches * PATCH
    n_out = len(pieces)

    def kernel(meta, adjoint, carried, trans, right, left, *refs):
        outs, refs = refs[:n_out], refs[n_out:]
        after, field, half, grid, out_sems = refs
        clear(grid)
        for p in range(patches):
            for k in range(PATCH // BSIDE):
                load = lambda ref, c: ref[at_rows(c, k), cols(p)].astype(F32)
                back_step(
                    meta,
                    p,
                    k,
                    (load(adjoint, 0), load(adjoint, 1)),
                    (load(carried, 0), load(carried, 1)),
                    (load(trans, 0) + 1.0, load(trans, 1)),
                    grid,
                    field,
                )
        copies = send_out(grid, outs, out_sems)
        propagate(field, half, right, left, patches, put_conjugate(after))
        for copy in copies:
            copy.wait()

    plane = jax.ShapeDtypeStruct((2 * PATCH, wide), BF16)
    strips = [jax.ShapeDtypeStruct((n, 2, BSIDE, TALL), BF16) for n in pieces]
    *outs, after = pl.pallas_call(
        kernel,
        out_shape=(*strips, plane),
        in_specs=[smem_spec()] + [vmem_spec()] * 5,
        out_specs=(*[any_spec()] * n_out, vmem_spec()),
        scratch_shapes=[
            pltpu.VMEM((wide, 2 * PATCH), BF16),
            pltpu.VMEM((2 * PATCH, wide), BF16),
            pltpu.VMEM((sum(pieces), 2, BSIDE, TALL), BF16),
            pltpu.SemaphoreType.DMA((n_out,)),
        ],
        compiler_params=params(),
        cost_estimate=cost(2.3),
        name=f"backward_{layer}",
    )(meta, adjoint, carried, trans, right, left)
    return outs, after


def first_slice(meta, adjoint, probe, trans, pieces, patches):
    wide = patches * PATCH
    n_out = len(pieces)

    def kernel(meta, adjoint, probe, trans, *refs):
        outs, refs = refs[:n_out], refs[n_out:]
        total, field, grid, out_sems = refs
        clear(grid)
        for p in range(patches):
            for k in range(PATCH // BSIDE):
                load = lambda ref, c: ref[at_rows(c, k), cols(p)].astype(F32)
                gr, gi = load(adjoint, 0), load(adjoint, 1)
                tr, ti = load(trans, 0) + 1.0, load(trans, 1)
                pr, pi = probe[p, 0, rows(k), :], probe[p, 1, rows(k), :]
                add_gradient(meta, grid, p, k, (gr * pr + gi * pi, gi * pr - gr * pi))
                field[at_rows(p, k), cols(0)] = (gr * tr + gi * ti).astype(BF16)
                field[at_rows(p, k), cols(1)] = (gi * tr - gr * ti).astype(BF16)
        copies = send_out(grid, outs, out_sems)
        moves = [shifts(meta, p) for p in range(patches)]
        for c in range(2):
            terms = [
                dot(dot_nt(my, field[cols(p), cols(c)]).astype(BF16), mx)
                for p, (my, mx) in enumerate(moves)
            ]
            total[c] = sum(terms[1:], terms[0]).astype(BF16)
        for copy in copies:
            copy.wait()

    strips = [jax.ShapeDtypeStruct((n, 2, BSIDE, TALL), BF16) for n in pieces]
    *outs, total = pl.pallas_call(
        kernel,
        out_shape=(*strips, jax.ShapeDtypeStruct((2, PATCH, PATCH), BF16)),
        in_specs=[smem_spec()] + [vmem_spec()] * 3,
        out_specs=(*[any_spec()] * n_out, vmem_spec()),
        scratch_shapes=[
            pltpu.VMEM((wide, 2 * PATCH), BF16),
            pltpu.VMEM((sum(pieces), 2, BSIDE, TALL), BF16),
            pltpu.SemaphoreType.DMA((n_out,)),
        ],
        compiler_params=params(),
        cost_estimate=cost(2.3),
        name="first_slice",
    )(meta, adjoint, probe, trans)
    return outs, total


def lane_group(shape):
    return lax.broadcasted_iota(jnp.int32, shape, 1) // BSIDE


def to_strips(blocks):
    flat = blocks.reshape(-1, BSIDE * BSIDE)

    def kernel(flat, *refs):
        outs, lanes = refs[:-1], refs[-1]
        group = lane_group((8, 128))
        for ag in range(8):
            lanes[ag] = flat[:, ag * 128 : (ag + 1) * 128]
        for s in range(SLICES):
            for t in range(2):
                tall = []
                for ag in range(8):
                    chunk = [
                        lanes[ag, pl.ds(t * 128 + band * 8 + 2 * s + c, 8, stride=16), :]
                        for band in range(2)
                        for c in range(2)
                    ]
                    for a4 in range(4):
                        value = None
                        for n in range(4):
                            move = (n - a4) % 4 * BSIDE
                            moved = pltpu.roll(chunk[n], move, 1) if move else chunk[n]
                            value = moved if n == 0 else jnp.where(group == n, moved, value)
                        tall.append(value)
                for half in range(2):
                    square = jnp.concatenate(tall[half * 16 : half * 16 + 16], axis=0)
                    square = jnp.transpose(square).astype(BF16)
                    for n in range(4):
                        outs[s][n // 2, n % 2, :, pl.ds(t * PATCH + half * 128, 128)] = square[
                            n * BSIDE : (n + 1) * BSIDE
                        ]

    return pl.pallas_call(
        kernel,
        out_shape=[jax.ShapeDtypeStruct((2, 2, BSIDE, TALL), BF16)] * SLICES,
        in_specs=[vmem_spec()],
        out_specs=[vmem_spec()] * SLICES,
        scratch_shapes=[pltpu.VMEM((8, flat.shape[0], 128), F32)],
        compiler_params=params(),
        cost_estimate=cost(1.5),
        name="to_strips",
    )(flat)


def to_blocks(terms):
    counts = [len(term) for term in terms]

    def kernel(*refs):
        out, lanes = refs[-2:]
        group = lane_group((8, 128))
        start = 0
        for s in range(SLICES):
            parts = refs[start : start + counts[s]]
            start += counts[s]
            for t in range(2):
                for half in range(2):
                    pieces = []
                    for n in range(4):
                        spot = (n // 2, n % 2, slice(None), pl.ds(t * PATCH + half * 128, 128))
                        value = parts[0][spot].astype(F32)
                        for part in parts[1:]:
                            value = value + part[spot].astype(F32)
                        pieces.append(value)
                    tall = jnp.transpose(jnp.concatenate(pieces, axis=0))
                    for g in range(4):
                        chunk = [tall[(g * 4 + a4) * 8 : (g * 4 + a4) * 8 + 8] for a4 in range(4)]
                        ag = half * 4 + g
                        for n in range(4):
                            value = None
                            for a4 in range(4):
                                move = (a4 - n) % 4 * BSIDE
                                moved = pltpu.roll(chunk[a4], move, 1) if move else chunk[a4]
                                value = moved if a4 == 0 else jnp.where(group == a4, moved, value)
                            row = t * 128 + n // 2 * 8 + 2 * s + n % 2
                            lanes[ag, pl.ds(row, 8, stride=16), :] = value
        for ag in range(8):
            out[:, ag * 128 : (ag + 1) * 128] = lanes[ag]

    flat = [part for term in terms for part in term]
    out = pl.pallas_call(
        kernel,
        out_shape=jax.ShapeDtypeStruct((FOOT * COL_BANDS * 2 * SLICES, BSIDE * BSIDE), F32),
        in_specs=[vmem_spec()] * len(flat),
        out_specs=vmem_spec(),
        scratch_shapes=[pltpu.VMEM((8, FOOT * COL_BANDS * 2 * SLICES, 128), F32)],
        compiler_params=params(),
        cost_estimate=cost(1.5),
        name="to_blocks",
    )(*flat)
    return out.reshape(FOOT * COL_BANDS, 2 * SLICES, BSIDE * BSIDE)


def after(value, *events):
    return lax.optimization_barrier((value, *events))[0]


def describe(top, left, source_of, target_of, last):
    first = left // BSIDE
    strips = jnp.minimum(first[:, None] + jnp.arange(WIN, dtype=jnp.int32)[None, :], last)
    columns = [top[:, None], (left % BSIDE)[:, None], source_of(strips), target_of(strips)]
    return jnp.concatenate(columns, axis=1).astype(jnp.int32)


FAR, NEAR, OVER_Y, OVER_CORE = 8, 4, 2, 1


def swap(value, bit):
    return lax.ppermute(value, "scan", [(i, i ^ bit) for i in range(16)])


def stage(moves, *events):
    values = lax.optimization_barrier((*(value for value, _ in moves), *events))
    return [swap(value, bit) for value, (_, bit) in zip(values, moves)]


def join(*values):
    return jnp.concatenate(values, axis=0)


def widen(value):
    return value.astype(F32)


def plus(value, *others):
    return sum((widen(other) for other in others), widen(value)).astype(BF16)


def slots(owner, order):
    bits = [(owner & bit) // bit * 2**n for n, bit in enumerate(order)]
    return sum(bits[1:], bits[0])


LINE_FIRST = (FAR, NEAR, OVER_Y, OVER_CORE)
PLANE_FIRST = (OVER_Y, FAR, NEAR, OVER_CORE)


def sum_probe(total, n_terms, before_near, before_far, before_y):
    me = lax.axis_index("scan")
    core, y = me % 2, me // 2 % 2
    mine = jnp.where(core == 0, total[0], total[1])
    theirs = jnp.where(core == 0, total[1], total[0])
    mine = plus(mine, swap(theirs, OVER_CORE))
    mine = mine.reshape(2, PATCH // 2, PATCH)
    theirs = jnp.where(y == 0, mine[1], mine[0])
    mine = jnp.where(y == 0, mine[0], mine[1])
    mine = plus(mine, swap(theirs, OVER_Y))
    mine = plus(mine, swap(after(mine, before_near), NEAR))
    mine = (widen(mine) + widen(swap(after(mine, before_far), FAR))) / math.sqrt(n_terms)
    other = swap(after(mine, before_y), OVER_Y)
    mine = jnp.where(y == 0, join(mine, other), join(other, mine))
    other = swap(mine, OVER_CORE)
    return jnp.where(core == 0, jnp.stack([mine, other]), jnp.stack([other, mine]))


def on_small(object_blocks, probe, positions, anchors, amplitudes):
    me = lax.axis_index("scan")
    corner = anchors[0] * BSIDE
    patches = positions.shape[0]

    def described(order):
        def place(strips):
            return slots(strips % OWN_COLS ^ me, order) * COL_BANDS + strips // OWN_COLS

        return describe(
            positions[:, 0] + corner[0],
            positions[:, 1] + corner[1],
            place,
            place,
            OWN_COLS * COL_BANDS - 1,
        )

    meta, meta_last = described(LINE_FIRST), described(PLANE_FIRST)
    hr, hl, fl, fr = tables()
    own = to_strips(object_blocks)

    far0, ys = stage([(own[0], FAR), (join(*own), OVER_Y)])
    far1, near0 = stage([(join(own[1], own[3]), FAR), (join(own[0], far0), NEAR)])
    far1, far3 = far1[:2], far1[2:]
    far2, near1, y0 = stage(
        [(own[2], FAR), (join(own[1], far1), NEAR), (join(far0, near0), OVER_Y)],
        ys,
        meta,
        meta_last,
    )
    pair3 = join(own[3], ys[6:])
    here0 = join(own[0], far0, near0, ys[:2], y0)
    core0, near2, y1, far3y = stage(
        [
            (here0, OVER_CORE),
            (join(own[2], far2), NEAR),
            (join(far1, near1), OVER_Y),
            (ys[6:], FAR),
        ],
    )
    here1 = join(own[1], far1, near1, ys[2:4], y1)
    here3 = join(pair3, far3, far3y)
    core1, y2, near3 = stage(
        [(here1, OVER_CORE), (join(far2, near2), OVER_Y), (here3, NEAR)], core0
    )
    trans0, q1, probes = forward(0, meta, (here0, core0), probe, hr, hl, patches)
    trans1, q2 = forward(1, meta, (here1, core1), q1, hr, hl, patches)
    here2 = join(own[2], far2, near2, ys[4:6], y2)
    core3a = swap(after(here3, q1), OVER_CORE)
    core2 = swap(after(here2, q2), OVER_CORE)
    core3b = swap(near3, OVER_CORE)

    pieces = (8, 8, 16)
    (here2, over2, core2), (here3, near3, core3), g1 = turn(
        (meta, meta_last),
        ((here2, core2), (here3, near3, core3a, core3b)),
        q2,
        amplitudes,
        (hr, hl, fl, fr),
        pieces,
        patches,
    )

    came3 = swap(core3, OVER_CORE)
    came2 = swap(core2, OVER_CORE)
    near3 = plus(near3, came3[8:])
    (here1, over1, core1), g0 = backward(1, meta, g1, q1, trans1, hr, hl, pieces, patches)
    came1 = swap(core1, OVER_CORE)
    y2 = plus(over2[2:], came2[10:])
    y1 = plus(over1[2:], came1[10:])
    here3 = plus(here3, came3[:8])
    (here0, over0, core0), total = first_slice(
        meta, after(g0, y2, y1, near3), probes, trans0, pieces, patches
    )
    near3 = swap(near3, NEAR)
    y2 = swap(y2, OVER_Y)
    came0 = swap(core0, OVER_CORE)
    y0 = plus(over0[2:], came0[10:])
    line2 = plus(here2[2:], came2[2:8], y2)
    near2, y1, far3 = stage(
        [(line2[2:], NEAR), (y1, OVER_Y), (plus(here3[4:], near3[4:]), FAR)], y0
    )
    line1 = plus(here1[2:], came1[2:8], y1)
    far2, near1, y0 = stage(
        [(plus(line2[:2], near2[2:]), FAR), (line1[2:], NEAR), (y0, OVER_Y)]
    )
    pair3 = plus(here3[:4], near3[:4], far3)
    line0 = plus(here0[2:], came0[2:8], y0)
    rest = [
        plus(over0[:2], came0[8:10]),
        plus(over1[:2], came1[8:10]),
        plus(over2[:2], came2[8:10]),
    ]
    far1, near0, ys = stage(
        [
            (plus(line1[:2], near1[2:]), FAR),
            (line0[2:], NEAR),
            (join(*rest, pair3[2:]), OVER_Y),
        ],
        far2,
    )
    far0 = swap(plus(line0[:2], near0[2:]), FAR)
    n_terms = lax.axis_size("scan") * patches
    probe_gradient = sum_probe(total, n_terms, near2, far2, near0)
    terms = [
        (plus(here0[:2], came0[:2]), near0[:2], ys[:2], far0),
        (plus(here1[:2], came1[:2]), near1[:2], ys[2:4], far1),
        (plus(here2[:2], came2[:2]), near2[:2], ys[4:6], far2),
        (pair3[:2], ys[6:]),
    ]
    return (to_blocks(terms), probe_gradient)


def footprint_slots(anchor_row, anchor_col, target, slot_number, own_rows):
    per_col = FOOT // OWN_COLS
    first_row = (target // OWN_COLS - anchor_row) % own_rows
    first_col = (target % OWN_COLS - anchor_col) % OWN_COLS
    inner_row = first_row + own_rows * (slot_number // per_col)
    inner_col = first_col + OWN_COLS * (slot_number % per_col)
    row_block = anchor_row + inner_row
    col_block = anchor_col + inner_col
    local = row_block // own_rows * COL_BANDS + col_block // OWN_COLS
    return (inner_row * FOOT + inner_col, local)


def work(meta, sources, probe, amplitudes, pieces):
    patches = amplitudes.shape[0]
    hr, hl, fl, fr = tables()
    t0, q1, probes = forward(0, meta, sources[0], probe, hr, hl, patches)
    t1, q2 = forward(1, meta, sources[1], q1, hr, hl, patches)
    grad2, grad3, g1 = turn(
        (meta, meta), sources[2:], q2, amplitudes, (hr, hl, fl, fr), pieces, patches
    )
    grad1, g0 = backward(1, meta, g1, q1, t1, hr, hl, pieces, patches)
    grad0, total = first_slice(meta, g0, probes, t0, pieces, patches)
    return [grad0, grad1, grad2, grad3], total


def on_any(object_blocks, probe, positions, anchors, amplitudes):
    n_scan = lax.axis_size("scan")
    own_rows = n_scan // OWN_COLS
    capacity = FOOT * FOOT // n_scan
    per_col = FOOT // OWN_COLS
    channels = object_blocks.shape[1]
    anchor_row = anchors[0, 0]
    anchor_col = anchors[0, 1]
    targets = jnp.arange(n_scan, dtype=jnp.int32)[:, None]
    slots = jnp.arange(capacity, dtype=jnp.int32)[None, :]
    send_order, wanted = footprint_slots(anchor_row, anchor_col, targets, slots, own_rows)
    inner = jnp.arange(FOOT, dtype=jnp.int32)
    inner_row = inner[:, None]
    inner_col = inner[None, :]
    holder = (anchor_row + inner_row) % own_rows * OWN_COLS + (anchor_col + inner_col) % OWN_COLS
    arrival = (holder * capacity + inner_row // own_rows * per_col + inner_col // OWN_COLS).reshape(
        -1
    )
    stored = object_blocks.astype(BF16)
    asked = lax.all_to_all(wanted, "scan", split_axis=0, concat_axis=0, tiled=True)
    found = jnp.take(stored, asked, axis=0)
    received = lax.all_to_all(found, "scan", split_axis=0, concat_axis=0, tiled=True)
    footprint = jnp.take(
        received.reshape(n_scan * capacity, channels, BSIDE * BSIDE), arrival, axis=0
    )
    strips = (
        footprint.reshape(2, 8, FOOT, SLICES, 2, BSIDE, BSIDE)
        .transpose(3, 2, 4, 6, 0, 5, 1)
        .reshape(SLICES, FOOT, 2, BSIDE, TALL)
    )
    meta = describe(
        positions[:, 0], positions[:, 1], lambda strips: strips, lambda strips: strips, FOOT - 1
    )
    sources = [(strips[s],) for s in range(SLICES)]
    grads, total = work(meta, sources, probe, amplitudes, (FOOT,))
    blocked = (
        jnp.stack([grad[0] for grad in grads])
        .reshape(SLICES, FOOT, 2, BSIDE, 2, BSIDE, 8)
        .transpose(4, 6, 1, 0, 2, 5, 3)
        .reshape(FOOT * FOOT, channels, BSIDE * BSIDE)
    )
    outgoing = jnp.take(blocked, send_order.reshape(-1), axis=0).reshape(
        n_scan, capacity, channels, BSIDE * BSIDE
    )
    incoming = lax.all_to_all(outgoing, "scan", split_axis=0, concat_axis=0, tiled=True)
    owned = jnp.arange(object_blocks.shape[0], dtype=jnp.int32)
    selector = (asked.reshape(-1)[:, None] == owned[None, :]).astype(F32)
    object_gradient = jnp.einsum(
        "sk,scb->kcb",
        selector,
        incoming.reshape(n_scan * capacity, channels, BSIDE * BSIDE).astype(F32),
        precision=lax.Precision.HIGHEST,
    )
    summed = lax.psum(widen(total), "scan")
    return (object_gradient, summed / math.sqrt(n_scan * positions.shape[0]))


def solution(mesh):
    in_specs = (
        P(("group", "scan"), None, None),
        P("group", None, None),
        P(("group", "scan"), None),
        P(("group", "scan"), None),
        P(("group", "scan"), None, None),
    )
    out_specs = (P(("group", "scan"), None, None), P("group", None, None))
    small = mesh.shape["scan"] == OWN_COLS
    return jax.shard_map(
        on_small if small else on_any,
        mesh=mesh,
        in_specs=in_specs,
        out_specs=out_specs,
        check_vma=False,
    )
```

```python
import math

import jax
import jax.numpy as jnp
import numpy as np
from jax import lax
from jax.experimental import pallas as pl
from jax.experimental.pallas import tpu as pltpu
from jax.sharding import PartitionSpec as P

PATCH = 256
SLICES = 4
BSIDE = 32
FOOT = 16
OWN_COLS = 16
COL_BANDS = 2
FLOOR = 0.25
WIN = 9
TALL = FOOT * BSIDE
VMEM_BYTES = 16 * 1024 * 1024
SCALE = 3.6e6
F32 = jnp.float32
BF16 = jnp.bfloat16


def lane_rows():
    lane = np.arange(PATCH)
    return lane % 8 * BSIDE + lane // 8


def stacked_right(table):
    real, imag = table
    return np.block([[real, imag], [-imag, real]])


def stacked_left(table):
    real, imag = table
    return np.block([[real, -imag], [imag, real]])


def tables():
    counter = np.arange(PATCH)
    turns = counter[:, None] * counter[None, :] % PATCH
    angles = turns.astype(np.float64) * (2.0 * math.pi / PATCH)
    scaled = 1.0 / math.sqrt(PATCH)
    dft = (np.cos(angles) * scaled, -np.sin(angles) * scaled)
    centred = (counter + PATCH // 2) % PATCH - PATCH // 2
    turns = (4 * counter[:, None] * counter[None, :] - centred[None, :] ** 2) % (4 * PATCH)
    angles = turns.astype(np.float64) * (2.0 * math.pi / (4 * PATCH))
    gap = (counter[:, None] - counter[None, :]) % PATCH
    fresnel = ((np.cos(angles).sum(1) / PATCH)[gap], (np.sin(angles).sum(1) / PATCH)[gap])
    order = lane_rows()
    across = tuple(part.T[np.ix_(order, order)] for part in fresnel)
    down = tuple(part.T for part in fresnel)
    wanted = (
        stacked_right(across),
        stacked_left(down),
        stacked_left(dft),
        stacked_right(dft),
    )
    return tuple(jnp.asarray(t.astype(np.float32)).astype(BF16) for t in wanted)


def dot(left, right):
    return jnp.dot(left, right, preferred_element_type=F32)


def dot_nt(left, right):
    return lax.dot_general(left, right, (((1,), (1,)), ((), ())), preferred_element_type=F32)


def row_of_lane(shape):
    lane = lax.broadcasted_iota(jnp.int32, shape, 1)
    return (lane & 7) * BSIDE + (lane >> 3)


def shifts(meta, p, dtype=BF16):
    top, left = meta[p, 0], meta[p, 1]
    shape = (PATCH, PATCH)
    i = lax.broadcasted_iota(jnp.int32, shape, 0)
    j = lax.broadcasted_iota(jnp.int32, shape, 1)
    my = jnp.where(row_of_lane(shape) == ((i + top) & (PATCH - 1)), 1.0, 0.0).astype(dtype)
    mx = jnp.where(i == ((j + left) & (PATCH - 1)), 1.0, 0.0).astype(dtype)
    return my, mx


def cols(c):
    return pl.ds(c * PATCH, PATCH)


def strip_copy(source, place, window, sems, p, k):
    return pltpu.make_async_copy(source.at[place], window.at[p, k], sems.at[p, k])


def fetch(meta, sources, window, sems, patches):
    per = sources[0].shape[0]
    for p in range(patches):
        for k in range(WIN):
            place = meta[p, 2 + k]
            for m, source in enumerate(sources):

                @pl.when(place // per == m)
                def _(source=source, place=place - m * per, p=p, k=k):
                    strip_copy(source, place, window, sems, p, k).start()


def await_fetch(sources, window, sems, patches):
    for p in range(patches):
        for k in range(WIN):
            strip_copy(sources[0], 0, window, sems, p, k).wait()


def patch_rows(meta, window, p, k):
    top, left = meta[p, 0], meta[p, 1]
    low = row_of_lane((BSIDE, PATCH)) < top
    out = []
    for c in range(2):

        def pick(slot):
            strip = window[p, slot, c].astype(F32)
            return jnp.where(low, strip[:, PATCH:], strip[:, :PATCH])

        value = pick(k)
        if k == 0:
            b = lax.broadcasted_iota(jnp.int32, (BSIDE, PATCH), 0)
            value = jnp.where(b < left, pick(WIN - 1), value)
        out.append(value)
    return out


def propagate(field, half, right, left, patches, put):
    for p in range(patches):
        y = dot(field[cols(p), :], right[...])
        for c in range(2):
            half[cols(c), cols(p)] = y[:, c * PATCH : (c + 1) * PATCH].astype(BF16)
    for c in range(2):
        put(c, dot(left[cols(c), :], half[...]))


def add_gradient(meta, grid, p, k, pair):
    top, left = meta[p, 0], meta[p, 1]
    low = row_of_lane((BSIDE, PATCH)) < top
    b = lax.broadcasted_iota(jnp.int32, (BSIDE, PATCH), 0)

    def put(slot, c, value):
        place = meta[p, 2 + WIN + slot]
        for half in range(2):
            piece = jnp.where(low if half else jnp.logical_not(low), value, 0.0)
            spot = (place, c, slice(None), slice(half * PATCH, (half + 1) * PATCH))
            if p > 0 or slot == WIN - 1:
                piece = piece + grid[spot].astype(F32)
            grid[spot] = piece.astype(BF16)

    if k > 0:
        for c in range(2):
            put(k, c, pair[c])
        return
    for c in range(2):
        put(0, c, jnp.where(b < left, 0.0, pair[c]))

    @pl.when(left > 0)
    def _():
        for c in range(2):
            put(WIN - 1, c, jnp.where(b < left, pair[c], 0.0))


def send_out(grid, outs, sems):
    start = 0
    copies = []
    for n, out in enumerate(outs):
        size = out.shape[0]
        copies.append(pltpu.make_async_copy(grid.at[pl.ds(start, size)], out, sems.at[n]))
        start += size
    for copy in copies:
        copy.start()
    return copies


def rows(k):
    return pl.ds(k * BSIDE, BSIDE)


def at_rows(c, k):
    return pl.ds(c * PATCH + k * BSIDE, BSIDE)


def any_spec():
    return pl.BlockSpec(memory_space=pl.ANY)


def vmem_spec():
    return pl.BlockSpec(memory_space=pltpu.VMEM)


def smem_spec():
    return pl.BlockSpec(memory_space=pltpu.SMEM)


def params():
    return pltpu.CompilerParams(vmem_limit_bytes=VMEM_BYTES)


def cost(microseconds):
    return pl.CostEstimate(flops=0, bytes_accessed=int(microseconds * SCALE), transcendentals=0)


def wrap_exact(value, mx, my):
    high = value.astype(BF16)
    rest = value - high.astype(F32)
    middle = rest.astype(BF16)
    low = (rest - middle.astype(F32)).astype(BF16)
    high, middle, low = (dot(dot_nt(mx, part).astype(BF16), my) for part in (high, middle, low))
    return high + (middle + low)


def forward(layer, meta, sources, before, right, left, patches):
    wide = patches * PATCH

    n = len(sources)

    def kernel(meta, *refs):
        sources, (before, right, left, trans, after), refs = refs[:n], refs[n : n + 5], refs[n + 5 :]
        fetch(meta, sources, window := refs[-4], sems := refs[-1], patches)
        field, half = refs[-3:-1]
        if layer == 0:
            probe, before = before, refs[0]
            for p in range(patches):
                my, mx = shifts(meta, p)
                for c in range(2):
                    before[p, c] = wrap_exact(probe[c], mx, my)
        await_fetch(sources, window, sems, patches)
        for p in range(patches):
            for k in range(PATCH // BSIDE):
                tr, ti = patch_rows(meta, window, p, k)
                trans[at_rows(0, k), cols(p)] = tr.astype(BF16)
                trans[at_rows(1, k), cols(p)] = ti.astype(BF16)
                tr = tr + 1.0
                if layer == 0:
                    fr, fi = before[p, 0, rows(k), :], before[p, 1, rows(k), :]
                else:
                    fr = before[at_rows(0, k), cols(p)].astype(F32)
                    fi = before[at_rows(1, k), cols(p)].astype(F32)
                field[at_rows(p, k), cols(0)] = (tr * fr - ti * fi).astype(BF16)
                field[at_rows(p, k), cols(1)] = (tr * fi + ti * fr).astype(BF16)

        def put(c, value):
            after[cols(c), :] = value.astype(BF16)

        propagate(field, half, right, left, patches, put)

    plane = jax.ShapeDtypeStruct((2 * PATCH, wide), BF16)
    extra = [jax.ShapeDtypeStruct((patches, 2, PATCH, PATCH), F32)] if layer == 0 else []
    return pl.pallas_call(
        kernel,
        out_shape=[plane, plane, *extra],
        in_specs=[smem_spec()] + [any_spec()] * n + [vmem_spec()] * 3,
        out_specs=[vmem_spec()] * (2 + len(extra)),
        scratch_shapes=[
            pltpu.VMEM((patches, WIN, 2, BSIDE, TALL), BF16),
            pltpu.VMEM((wide, 2 * PATCH), BF16),
            pltpu.VMEM((2 * PATCH, wide), BF16),
            pltpu.SemaphoreType.DMA((patches, WIN)),
        ],
        compiler_params=params(),
        cost_estimate=cost(3.5),
        name=f"forward_{layer}",
    )(meta, *sources, before, right, left)


def back_step(meta, p, k, g, q, t, grid, field):
    gr, gi = g
    qr, qi = q
    tr, ti = t
    add_gradient(meta, grid, p, k, (gr * qr + gi * qi, gi * qr - gr * qi))
    field[at_rows(p, k), cols(0)] = (tr * gr + ti * gi).astype(BF16)
    field[at_rows(p, k), cols(1)] = (ti * gr - tr * gi).astype(BF16)


def clear(grid):
    @pl.loop(0, grid.shape[0])
    def _(n):
        grid[n] = jnp.zeros(grid.shape[1:], BF16)


def put_conjugate(out):
    def put(c, value):
        out[cols(c), :] = (-value if c else value).astype(BF16)

    return put


def through_slice(meta, window, load, trans, field, patches):
    for p in range(patches):
        for k in range(PATCH // BSIDE):
            tr, ti = patch_rows(meta, window, p, k)
            trans[at_rows(0, k), cols(p)] = tr.astype(BF16)
            trans[at_rows(1, k), cols(p)] = ti.astype(BF16)
            tr = tr + 1.0
            fr, fi = load(p, 0, k), load(p, 1, k)
            field[at_rows(p, k), cols(0)] = (tr * fr - ti * fi).astype(BF16)
            field[at_rows(p, k), cols(1)] = (tr * fi + ti * fr).astype(BF16)


def loader(ref):
    return lambda p, c, k: ref[at_rows(c, k), cols(p)].astype(F32)


def put_plain(out):
    def put(c, value):
        out[cols(c), :] = value.astype(BF16)

    return put


def dft_pair(half, other, left, right, patches, use):
    for c in range(2):
        y = dot(left[cols(c), :], half[...])
        for p in range(patches):
            other[cols(p), cols(c)] = y[:, p * PATCH : (p + 1) * PATCH].astype(BF16)
    for p in range(patches):
        use(p, dot(other[cols(p), :], right[...]))


def turn(metas, groups, carried, amplitudes, tabs, pieces, patches):
    wide = patches * PATCH
    n_out = len(pieces)
    n2, n3 = len(groups[0]), len(groups[1])

    def kernel(meta, meta_last, *refs):
        given2, given3, refs = refs[:n2], refs[n2 : n2 + n3], refs[n2 + n3 :]
        q2, measured, hr, hl, fl, fr = refs[:6]
        outs, refs = refs[6 : 6 + 2 * n_out], refs[6 + 2 * n_out :]
        after, windows, t2, t3, q3, adjoint, field, half, other, grids, sems, out_sems = refs
        fetch(meta, given2, windows.at[0], sems.at[0], patches)
        fetch(meta_last, given3, windows.at[1], sems.at[1], patches)
        clear(grids.at[0])
        clear(grids.at[1])
        await_fetch(given2, windows.at[0], sems.at[0], patches)
        through_slice(meta, windows.at[0], loader(q2), t2, field, patches)
        propagate(field, half, hr, hl, patches, put_plain(q3))
        await_fetch(given3, windows.at[1], sems.at[1], patches)
        through_slice(meta_last, windows.at[1], loader(q3), t3, field, patches)
        moves = [shifts(meta, p) for p in range(patches)]
        for p, (my, mx) in enumerate(moves):
            for c in range(2):
                turned = dot_nt(my, field[cols(p), cols(c)]).astype(BF16)
                half[cols(c), cols(p)] = dot(turned, mx).astype(BF16)

        def misfit(p, far):
            real, imag = far[:, :PATCH], far[:, PATCH:]
            modulus = jnp.sqrt(real * real + imag * imag)
            keeping = 1.0 - measured[p] / jnp.maximum(modulus, FLOOR)
            half[cols(0), cols(p)] = (real * keeping).astype(BF16)
            half[cols(1), cols(p)] = (-imag * keeping).astype(BF16)

        def wrapped(p, g):
            my, mx = moves[p]
            for c in range(2):
                part = g[:, c * PATCH : (c + 1) * PATCH]
                part = (-part if c else part).astype(BF16)
                adjoint[cols(c), cols(p)] = dot(dot_nt(mx, part).astype(BF16), my).astype(BF16)

        dft_pair(half, other, fl, fr, patches, misfit)
        dft_pair(half, other, fl, fr, patches, wrapped)

        def copies(layer):
            found, start = [], 0
            for n, size in enumerate(pieces):
                found.append(
                    pltpu.make_async_copy(
                        grids.at[layer, pl.ds(start, size)],
                        outs[layer * n_out + n],
                        out_sems.at[layer, n],
                    )
                )
                start += size
            return found

        g = loader(adjoint)
        for layer, spot, q, t, nxt in (
            (1, meta_last, loader(q3), loader(t3), adjoint),
            (0, meta, loader(q2), loader(t2), after),
        ):
            for p in range(patches):
                for k in range(PATCH // BSIDE):
                    back_step(
                        spot,
                        p,
                        k,
                        (g(p, 0, k), g(p, 1, k)),
                        (q(p, 0, k), q(p, 1, k)),
                        (t(p, 0, k) + 1.0, t(p, 1, k)),
                        grids.at[layer],
                        field,
                    )
            for copy in copies(layer):
                copy.start()
            propagate(field, half, hr, hl, patches, put_conjugate(nxt))
        for layer in range(2):
            for copy in copies(layer):
                copy.wait()

    plane = pltpu.VMEM((2 * PATCH, wide), BF16)
    strips = [jax.ShapeDtypeStruct((n, 2, BSIDE, TALL), BF16) for n in pieces]
    *outs, after = pl.pallas_call(
        kernel,
        out_shape=(*strips * 2, jax.ShapeDtypeStruct((2 * PATCH, wide), BF16)),
        in_specs=[smem_spec()] * 2 + [any_spec()] * (n2 + n3) + [vmem_spec()] * 6,
        out_specs=(*[any_spec()] * (2 * n_out), vmem_spec()),
        scratch_shapes=[
            pltpu.VMEM((2, patches, WIN, 2, BSIDE, TALL), BF16),
            plane,
            plane,
            plane,
            plane,
            pltpu.VMEM((wide, 2 * PATCH), BF16),
            plane,
            pltpu.VMEM((wide, 2 * PATCH), BF16),
            pltpu.VMEM((2, sum(pieces), 2, BSIDE, TALL), BF16),
            pltpu.SemaphoreType.DMA((2, patches, WIN)),
            pltpu.SemaphoreType.DMA((2, n_out)),
        ],
        compiler_params=params(),
        cost_estimate=cost(11.5),
        name="turn",
    )(*metas, *groups[0], *groups[1], carried, amplitudes, *tabs)
    return outs[:n_out], outs[n_out:], after


def backward(layer, meta, adjoint, carried, trans, right, left, pieces, patches):
    wide = patches * PATCH
    n_out = len(pieces)

    def kernel(meta, adjoint, carried, trans, right, left, *refs):
        outs, refs = refs[:n_out], refs[n_out:]
        after, field, half, grid, out_sems = refs
        clear(grid)
        for p in range(patches):
            for k in range(PATCH // BSIDE):
                load = lambda ref, c: ref[at_rows(c, k), cols(p)].astype(F32)
                back_step(
                    meta,
                    p,
                    k,
                    (load(adjoint, 0), load(adjoint, 1)),
                    (load(carried, 0), load(carried, 1)),
                    (load(trans, 0) + 1.0, load(trans, 1)),
                    grid,
                    field,
                )
        copies = send_out(grid, outs, out_sems)
        propagate(field, half, right, left, patches, put_conjugate(after))
        for copy in copies:
            copy.wait()

    plane = jax.ShapeDtypeStruct((2 * PATCH, wide), BF16)
    strips = [jax.ShapeDtypeStruct((n, 2, BSIDE, TALL), BF16) for n in pieces]
    *outs, after = pl.pallas_call(
        kernel,
        out_shape=(*strips, plane),
        in_specs=[smem_spec()] + [vmem_spec()] * 5,
        out_specs=(*[any_spec()] * n_out, vmem_spec()),
        scratch_shapes=[
            pltpu.VMEM((wide, 2 * PATCH), BF16),
            pltpu.VMEM((2 * PATCH, wide), BF16),
            pltpu.VMEM((sum(pieces), 2, BSIDE, TALL), BF16),
            pltpu.SemaphoreType.DMA((n_out,)),
        ],
        compiler_params=params(),
        cost_estimate=cost(2.3),
        name=f"backward_{layer}",
    )(meta, adjoint, carried, trans, right, left)
    return outs, after


def first_slice(meta, adjoint, probe, trans, pieces, patches):
    wide = patches * PATCH
    n_out = len(pieces)

    def kernel(meta, adjoint, probe, trans, *refs):
        outs, refs = refs[:n_out], refs[n_out:]
        total, field, grid, out_sems = refs
        clear(grid)
        for p in range(patches):
            for k in range(PATCH // BSIDE):
                load = lambda ref, c: ref[at_rows(c, k), cols(p)].astype(F32)
                gr, gi = load(adjoint, 0), load(adjoint, 1)
                tr, ti = load(trans, 0) + 1.0, load(trans, 1)
                pr, pi = probe[p, 0, rows(k), :], probe[p, 1, rows(k), :]
                add_gradient(meta, grid, p, k, (gr * pr + gi * pi, gi * pr - gr * pi))
                field[at_rows(p, k), cols(0)] = (gr * tr + gi * ti).astype(BF16)
                field[at_rows(p, k), cols(1)] = (gi * tr - gr * ti).astype(BF16)
        copies = send_out(grid, outs, out_sems)
        moves = [shifts(meta, p) for p in range(patches)]
        for c in range(2):
            terms = [
                dot(dot_nt(my, field[cols(p), cols(c)]).astype(BF16), mx)
                for p, (my, mx) in enumerate(moves)
            ]
            total[c] = sum(terms[1:], terms[0]).astype(BF16)
        for copy in copies:
            copy.wait()

    strips = [jax.ShapeDtypeStruct((n, 2, BSIDE, TALL), BF16) for n in pieces]
    *outs, total = pl.pallas_call(
        kernel,
        out_shape=(*strips, jax.ShapeDtypeStruct((2, PATCH, PATCH), BF16)),
        in_specs=[smem_spec()] + [vmem_spec()] * 3,
        out_specs=(*[any_spec()] * n_out, vmem_spec()),
        scratch_shapes=[
            pltpu.VMEM((wide, 2 * PATCH), BF16),
            pltpu.VMEM((sum(pieces), 2, BSIDE, TALL), BF16),
            pltpu.SemaphoreType.DMA((n_out,)),
        ],
        compiler_params=params(),
        cost_estimate=cost(2.3),
        name="first_slice",
    )(meta, adjoint, probe, trans)
    return outs, total


def lane_group(shape):
    return lax.broadcasted_iota(jnp.int32, shape, 1) // BSIDE


def to_strips(blocks):
    flat = blocks.reshape(-1, BSIDE * BSIDE)

    def kernel(flat, *refs):
        outs, lanes = refs[:-1], refs[-1]
        group = lane_group((8, 128))
        for ag in range(8):
            lanes[ag] = flat[:, ag * 128 : (ag + 1) * 128]
        for s in range(SLICES):
            for t in range(2):
                tall = []
                for ag in range(8):
                    chunk = [
                        lanes[ag, pl.ds(t * 128 + band * 8 + 2 * s + c, 8, stride=16), :]
                        for band in range(2)
                        for c in range(2)
                    ]
                    for a4 in range(4):
                        value = None
                        for n in range(4):
                            move = (n - a4) % 4 * BSIDE
                            moved = pltpu.roll(chunk[n], move, 1) if move else chunk[n]
                            value = moved if n == 0 else jnp.where(group == n, moved, value)
                        tall.append(value)
                for half in range(2):
                    square = jnp.concatenate(tall[half * 16 : half * 16 + 16], axis=0)
                    square = jnp.transpose(square).astype(BF16)
                    for n in range(4):
                        outs[s][n // 2, n % 2, :, pl.ds(t * PATCH + half * 128, 128)] = square[
                            n * BSIDE : (n + 1) * BSIDE
                        ]

    return pl.pallas_call(
        kernel,
        out_shape=[jax.ShapeDtypeStruct((2, 2, BSIDE, TALL), BF16)] * SLICES,
        in_specs=[vmem_spec()],
        out_specs=[vmem_spec()] * SLICES,
        scratch_shapes=[pltpu.VMEM((8, flat.shape[0], 128), F32)],
        compiler_params=params(),
        cost_estimate=cost(1.5),
        name="to_strips",
    )(flat)


def to_blocks(terms):
    counts = [len(term) for term in terms]

    def kernel(*refs):
        out, lanes = refs[-2:]
        group = lane_group((8, 128))
        start = 0
        for s in range(SLICES):
            parts = refs[start : start + counts[s]]
            start += counts[s]
            for t in range(2):
                for half in range(2):
                    pieces = []
                    for n in range(4):
                        spot = (n // 2, n % 2, slice(None), pl.ds(t * PATCH + half * 128, 128))
                        value = parts[0][spot].astype(F32)
                        for part in parts[1:]:
                            value = value + part[spot].astype(F32)
                        pieces.append(value)
                    tall = jnp.transpose(jnp.concatenate(pieces, axis=0))
                    for g in range(4):
                        chunk = [tall[(g * 4 + a4) * 8 : (g * 4 + a4) * 8 + 8] for a4 in range(4)]
                        ag = half * 4 + g
                        for n in range(4):
                            value = None
                            for a4 in range(4):
                                move = (a4 - n) % 4 * BSIDE
                                moved = pltpu.roll(chunk[a4], move, 1) if move else chunk[a4]
                                value = moved if a4 == 0 else jnp.where(group == a4, moved, value)
                            row = t * 128 + n // 2 * 8 + 2 * s + n % 2
                            lanes[ag, pl.ds(row, 8, stride=16), :] = value
        for ag in range(8):
            out[:, ag * 128 : (ag + 1) * 128] = lanes[ag]

    flat = [part for term in terms for part in term]
    out = pl.pallas_call(
        kernel,
        out_shape=jax.ShapeDtypeStruct((FOOT * COL_BANDS * 2 * SLICES, BSIDE * BSIDE), F32),
        in_specs=[vmem_spec()] * len(flat),
        out_specs=vmem_spec(),
        scratch_shapes=[pltpu.VMEM((8, FOOT * COL_BANDS * 2 * SLICES, 128), F32)],
        compiler_params=params(),
        cost_estimate=cost(1.5),
        name="to_blocks",
    )(*flat)
    return out.reshape(FOOT * COL_BANDS, 2 * SLICES, BSIDE * BSIDE)


def after(value, *events):
    return lax.optimization_barrier((value, *events))[0]


def describe(top, left, source_of, target_of, last):
    first = left // BSIDE
    strips = jnp.minimum(first[:, None] + jnp.arange(WIN, dtype=jnp.int32)[None, :], last)
    columns = [top[:, None], (left % BSIDE)[:, None], source_of(strips), target_of(strips)]
    return jnp.concatenate(columns, axis=1).astype(jnp.int32)


FAR, NEAR, OVER_Y, OVER_CORE = 8, 4, 2, 1


def swap(value, bit):
    return lax.ppermute(value, "scan", [(i, i ^ bit) for i in range(16)])


def stage(moves, *events):
    values = lax.optimization_barrier((*(value for value, _ in moves), *events))
    return [swap(value, bit) for value, (_, bit) in zip(values, moves)]


def join(*values):
    return jnp.concatenate(values, axis=0)


def widen(value):
    return value.astype(F32)


def plus(value, *others):
    return sum((widen(other) for other in others), widen(value)).astype(BF16)


def slots(owner, order):
    bits = [(owner & bit) // bit * 2**n for n, bit in enumerate(order)]
    return sum(bits[1:], bits[0])


LINE_FIRST = (FAR, NEAR, OVER_Y, OVER_CORE)
PLANE_FIRST = (OVER_Y, FAR, NEAR, OVER_CORE)


def sum_probe(total, n_terms, before_near, before_far, before_y):
    me = lax.axis_index("scan")
    core, y = me % 2, me // 2 % 2
    mine = jnp.where(core == 0, total[0], total[1])
    theirs = jnp.where(core == 0, total[1], total[0])
    mine = plus(mine, swap(theirs, OVER_CORE))
    mine = mine.reshape(2, PATCH // 2, PATCH)
    theirs = jnp.where(y == 0, mine[1], mine[0])
    mine = jnp.where(y == 0, mine[0], mine[1])
    mine = plus(mine, swap(theirs, OVER_Y))
    mine = plus(mine, swap(after(mine, before_near), NEAR))
    mine = (widen(mine) + widen(swap(after(mine, before_far), FAR))) / math.sqrt(n_terms)
    other = swap(after(mine, before_y), OVER_Y)
    mine = jnp.where(y == 0, join(mine, other), join(other, mine))
    other = swap(mine, OVER_CORE)
    return jnp.where(core == 0, jnp.stack([mine, other]), jnp.stack([other, mine]))


def on_small(object_blocks, probe, positions, anchors, amplitudes):
    me = lax.axis_index("scan")
    corner = anchors[0] * BSIDE
    patches = positions.shape[0]

    def described(order):
        def place(strips):
            return slots(strips % OWN_COLS ^ me, order) * COL_BANDS + strips // OWN_COLS

        return describe(
            positions[:, 0] + corner[0],
            positions[:, 1] + corner[1],
            place,
            place,
            OWN_COLS * COL_BANDS - 1,
        )

    meta, meta_last = described(LINE_FIRST), described(PLANE_FIRST)
    hr, hl, fl, fr = tables()
    own = to_strips(object_blocks)

    far0, ys = stage([(own[0], FAR), (join(*own), OVER_Y)])
    far1, near0 = stage([(join(own[1], own[3]), FAR), (join(own[0], far0), NEAR)])
    far1, far3 = far1[:2], far1[2:]
    far2, near1, y0 = stage(
        [(own[2], FAR), (join(own[1], far1), NEAR), (join(far0, near0), OVER_Y)],
        ys,
        meta,
        meta_last,
    )
    pair3 = join(own[3], ys[6:])
    here0 = join(own[0], far0, near0, ys[:2], y0)
    core0, near2, y1, far3y = stage(
        [
            (here0, OVER_CORE),
            (join(own[2], far2), NEAR),
            (join(far1, near1), OVER_Y),
            (ys[6:], FAR),
        ],
    )
    here1 = join(own[1], far1, near1, ys[2:4], y1)
    here3 = join(pair3, far3, far3y)
    core1, y2, near3 = stage(
        [(here1, OVER_CORE), (join(far2, near2), OVER_Y), (here3, NEAR)], core0
    )
    trans0, q1, probes = forward(0, meta, (here0, core0), probe, hr, hl, patches)
    trans1, q2 = forward(1, meta, (here1, core1), q1, hr, hl, patches)
    here2 = join(own[2], far2, near2, ys[4:6], y2)
    core3a = swap(after(here3, q1), OVER_CORE)
    core2 = swap(after(here2, q2), OVER_CORE)
    core3b = swap(near3, OVER_CORE)

    pieces = (8, 8, 16)
    (here2, over2, core2), (here3, near3, core3), g1 = turn(
        (meta, meta_last),
        ((here2, core2), (here3, near3, core3a, core3b)),
        q2,
        amplitudes,
        (hr, hl, fl, fr),
        pieces,
        patches,
    )

    came3 = swap(core3, OVER_CORE)
    came2 = swap(core2, OVER_CORE)
    near3 = plus(near3, came3[8:])
    (here1, over1, core1), g0 = backward(1, meta, g1, q1, trans1, hr, hl, pieces, patches)
    came1 = swap(core1, OVER_CORE)
    y2 = plus(over2[2:], came2[10:])
    y1 = plus(over1[2:], came1[10:])
    here3 = plus(here3, came3[:8])
    (here0, over0, core0), total = first_slice(
        meta, after(g0, y2, y1, near3), probes, trans0, pieces, patches
    )
    near3 = swap(near3, NEAR)
    y2 = swap(y2, OVER_Y)
    came0 = swap(core0, OVER_CORE)
    y0 = plus(over0[2:], came0[10:])
    line2 = plus(here2[2:], came2[2:8], y2)
    near2, y1, far3 = stage(
        [(line2[2:], NEAR), (y1, OVER_Y), (plus(here3[4:], near3[4:]), FAR)], y0
    )
    line1 = plus(here1[2:], came1[2:8], y1)
    far2, near1, y0 = stage(
        [(plus(line2[:2], near2[2:]), FAR), (line1[2:], NEAR), (y0, OVER_Y)]
    )
    pair3 = plus(here3[:4], near3[:4], far3)
    line0 = plus(here0[2:], came0[2:8], y0)
    rest = [
        plus(over0[:2], came0[8:10]),
        plus(over1[:2], came1[8:10]),
        plus(over2[:2], came2[8:10]),
    ]
    far1, near0, ys = stage(
        [
            (plus(line1[:2], near1[2:]), FAR),
            (line0[2:], NEAR),
            (join(*rest, pair3[2:]), OVER_Y),
        ],
        far2,
    )
    far0 = swap(plus(line0[:2], near0[2:]), FAR)
    n_terms = lax.axis_size("scan") * patches
    probe_gradient = sum_probe(total, n_terms, near2, near1, near0)
    terms = [
        (plus(here0[:2], came0[:2]), near0[:2], ys[:2], far0),
        (plus(here1[:2], came1[:2]), near1[:2], ys[2:4], far1),
        (plus(here2[:2], came2[:2]), near2[:2], ys[4:6], far2),
        (pair3[:2], ys[6:]),
    ]
    return (to_blocks(terms), probe_gradient)


def footprint_slots(anchor_row, anchor_col, target, slot_number, own_rows):
    per_col = FOOT // OWN_COLS
    first_row = (target // OWN_COLS - anchor_row) % own_rows
    first_col = (target % OWN_COLS - anchor_col) % OWN_COLS
    inner_row = first_row + own_rows * (slot_number // per_col)
    inner_col = first_col + OWN_COLS * (slot_number % per_col)
    row_block = anchor_row + inner_row
    col_block = anchor_col + inner_col
    local = row_block // own_rows * COL_BANDS + col_block // OWN_COLS
    return (inner_row * FOOT + inner_col, local)


def work(meta, sources, probe, amplitudes, pieces):
    patches = amplitudes.shape[0]
    hr, hl, fl, fr = tables()
    t0, q1, probes = forward(0, meta, sources[0], probe, hr, hl, patches)
    t1, q2 = forward(1, meta, sources[1], q1, hr, hl, patches)
    grad2, grad3, g1 = turn(
        (meta, meta), sources[2:], q2, amplitudes, (hr, hl, fl, fr), pieces, patches
    )
    grad1, g0 = backward(1, meta, g1, q1, t1, hr, hl, pieces, patches)
    grad0, total = first_slice(meta, g0, probes, t0, pieces, patches)
    return [grad0, grad1, grad2, grad3], total


def on_any(object_blocks, probe, positions, anchors, amplitudes):
    n_scan = lax.axis_size("scan")
    own_rows = n_scan // OWN_COLS
    capacity = FOOT * FOOT // n_scan
    per_col = FOOT // OWN_COLS
    channels = object_blocks.shape[1]
    anchor_row = anchors[0, 0]
    anchor_col = anchors[0, 1]
    targets = jnp.arange(n_scan, dtype=jnp.int32)[:, None]
    slots = jnp.arange(capacity, dtype=jnp.int32)[None, :]
    send_order, wanted = footprint_slots(anchor_row, anchor_col, targets, slots, own_rows)
    inner = jnp.arange(FOOT, dtype=jnp.int32)
    inner_row = inner[:, None]
    inner_col = inner[None, :]
    holder = (anchor_row + inner_row) % own_rows * OWN_COLS + (anchor_col + inner_col) % OWN_COLS
    arrival = (holder * capacity + inner_row // own_rows * per_col + inner_col // OWN_COLS).reshape(
        -1
    )
    stored = object_blocks.astype(BF16)
    asked = lax.all_to_all(wanted, "scan", split_axis=0, concat_axis=0, tiled=True)
    found = jnp.take(stored, asked, axis=0)
    received = lax.all_to_all(found, "scan", split_axis=0, concat_axis=0, tiled=True)
    footprint = jnp.take(
        received.reshape(n_scan * capacity, channels, BSIDE * BSIDE), arrival, axis=0
    )
    strips = (
        footprint.reshape(2, 8, FOOT, SLICES, 2, BSIDE, BSIDE)
        .transpose(3, 2, 4, 6, 0, 5, 1)
        .reshape(SLICES, FOOT, 2, BSIDE, TALL)
    )
    meta = describe(
        positions[:, 0], positions[:, 1], lambda strips: strips, lambda strips: strips, FOOT - 1
    )
    sources = [(strips[s],) for s in range(SLICES)]
    grads, total = work(meta, sources, probe, amplitudes, (FOOT,))
    blocked = (
        jnp.stack([grad[0] for grad in grads])
        .reshape(SLICES, FOOT, 2, BSIDE, 2, BSIDE, 8)
        .transpose(4, 6, 1, 0, 2, 5, 3)
        .reshape(FOOT * FOOT, channels, BSIDE * BSIDE)
    )
    outgoing = jnp.take(blocked, send_order.reshape(-1), axis=0).reshape(
        n_scan, capacity, channels, BSIDE * BSIDE
    )
    incoming = lax.all_to_all(outgoing, "scan", split_axis=0, concat_axis=0, tiled=True)
    owned = jnp.arange(object_blocks.shape[0], dtype=jnp.int32)
    selector = (asked.reshape(-1)[:, None] == owned[None, :]).astype(F32)
    object_gradient = jnp.einsum(
        "sk,scb->kcb",
        selector,
        incoming.reshape(n_scan * capacity, channels, BSIDE * BSIDE).astype(F32),
        precision=lax.Precision.HIGHEST,
    )
    summed = lax.psum(widen(total), "scan")
    return (object_gradient, summed / math.sqrt(n_scan * positions.shape[0]))


def solution(mesh):
    in_specs = (
        P(("group", "scan"), None, None),
        P("group", None, None),
        P(("group", "scan"), None),
        P(("group", "scan"), None),
        P(("group", "scan"), None, None),
    )
    out_specs = (P(("group", "scan"), None, None), P("group", None, None))
    small = mesh.shape["scan"] == OWN_COLS
    return jax.shard_map(
        on_small if small else on_any,
        mesh=mesh,
        in_specs=in_specs,
        out_specs=out_specs,
        check_vma=False,
    )
```
